32 devices in a mesh: dp: 8 (over y, x, core), tensor: 4 (over z).
Axes of the slice: x: 2, y: 2, z: 4, core: 2. Of those that a mesh axis runs over, the one named last changes fastest.
Arguments:
- hidden_in: bfloat16 [8192, 2048], P('dp'), may hold values from -6 to 6
- norm_gain: float32 [2048], replicated, may hold values from 0.5 to 1.5
- z_weight: bfloat16 [2048, 4096], P(None, 'tensor'), may hold values from -0.125 to 0.125
- x_weight: bfloat16 [2048, 4096], P(None, 'tensor'), may hold values from -0.125 to 0.125
- bc_weight: bfloat16 [2048, 256], replicated, may hold values from -0.125 to 0.125
- dt_weight: bfloat16 [2048, 64], P(None, 'tensor'), may hold values from -0.125 to 0.125
- conv_x: float32 [4, 4096], P(None, 'tensor'), may hold values from -3 to 3
- conv_x_bias: float32 [4096], P('tensor'), may hold values from -3 to 3
- conv_bc: float32 [4, 256], replicated, may hold values from -3 to 3
- conv_bc_bias: float32 [256], replicated, may hold values from -3 to 3
- dt_bias: float32 [64], P('tensor'), may hold values from -7 to -3.5
- a_log: float32 [64], P('tensor'), may hold values from 0 to 2.1
- d_skip: float32 [64], P('tensor'), may hold values from 0.3 to 3.5, as said below
- gate_gain: float32 [4096], P('tensor'), may hold values from 0.5 to 1.5
- out_weight: bfloat16 [4096, 2048], P('tensor'), may hold values from -0.09375 to 0.09375
- cotangent: bfloat16 [8192, 2048], P('dp'), may hold values from -6 to 6
- segment_ids: int32 [8192], P('dp'), may hold values from 0 to 31, never falling along the last dimension, each value on 1 to 512 neighbouring positions
Outputs:
- output: float32 [8192, 2048], P('dp')
- input_grad: float32 [8192, 2048], P('dp')
- norm_gain_grad: float32 [2048], replicated
- z_weight_grad: float32 [2048, 4096], P('dp', 'tensor')
- x_weight_grad: float32 [2048, 4096], P('dp', 'tensor')
- bc_weight_grad: float32 [2048, 256], P('dp')
- dt_weight_grad: float32 [2048, 64], P('dp', 'tensor')
- conv_x_grad: float32 [4, 4096], P(None, 'tensor')
- conv_x_bias_grad: float32 [4096], P('tensor')
- conv_bc_grad: float32 [4, 256], replicated
- conv_bc_bias_grad: float32 [256], replicated
- dt_bias_grad: float32 [64], P('tensor')
- a_log_grad: float32 [64], P('tensor')
- d_skip_grad: float32 [64], P('tensor')
- gate_gain_grad: float32 [4096], P('tensor')
- out_weight_grad: float32 [4096, 2048], P('tensor', 'dp')
The draws below stay inside these ranges and needn't reach their ends.
Inputs may be any that keep to these rules, and one draw needn't show every extreme that they name: `segment_ids`: document numbers never fall along the tokens; a document has at most 512 tokens. `d_skip`: positive.
All inputs are finite; a program needn't handle non-finite values.
Results may differ from the reference program's by a relative error of at most 0.0092.
Values sent between devices are 32-bit elements; how exact they have to be, the bound alone decides.
No kernel may reach another device: no remote copies, remote signals or barrier semaphores. Data moves between devices by JAX's collectives and lax.ppermute only.
A program may use at most 192 MiB of HBM per device.

```python
import math
import jax
import jax.numpy as jnp
import numpy as np
from jax import lax

D = 2048
D_INNER = 4096
HEADS = 64
STATE = 128
CONV = 4
GROUP = 256
SEQ_LEN = 1024
TOKENS = 8192


def draw_d_skip(key, part):
    key = jax.random.fold_in(key, 7)
    ladder = jnp.arange(HEADS, dtype=jnp.float32) / HEADS
    baseline = 0.5 + 1.5 * ladder
    jitter = jax.random.uniform(key, (HEADS,), jnp.float32, 0.75, 1.25)
    return baseline * jitter


def with_spikes(drawn, stream_key, source, target, blocks, factor):
    def block_of(dim):
        return (jnp.arange(drawn.shape[dim]) // (drawn.shape[dim] // blocks)).reshape((-1,) + (1,) * (drawn.ndim - 1 - dim))

    one_side = jax.random.permutation(stream_key, blocks)[block_of(target)]
    far = (block_of(target) + blocks // 2) % blocks
    return jnp.where((block_of(source) == one_side) | (block_of(source) == far), factor * drawn, drawn)


def levels(stream_key, dims, split, low, largest):
    loudness = 1.0
    for dim, blocks in split:
        heights = jax.random.uniform(jax.random.fold_in(jax.random.fold_in(stream_key, 6), dim), (blocks,), jnp.float32, low / len(split), largest / len(split))
        loudness = loudness * jnp.repeat(jnp.exp(heights), dims[dim] // blocks).reshape((-1,) + (1,) * (len(dims) - 1 - dim))
    return loudness


def profile(number_of, total, most, skew):
    portions = [(1 << 20) // math.isqrt(grade ** skew) + 1 for grade in range(2, number_of + 1)]
    rest, given = total - most - (number_of - 1), [1] * (number_of - 1)
    while rest > 0:
        free = [i for i in range(number_of - 1) if given[i] < most]
        mass, left = sum([portions[i] for i in free]), rest
        for i in free:
            more = min(most - given[i], max(1, left * portions[i] // mass), rest)
            given[i] = given[i] + more
            rest = rest - more
    return np.array([most] + given)


def ragged_sizes(own_key, amount, total, most, skew):
    if amount == 2:
        one = jax.random.randint(own_key, (), max(1, total - most), min(most, total - 1) + 1)
        return jnp.stack([one, total - one])
    tallies = jnp.asarray(profile(amount, total, most, skew), jnp.int32)
    twos = (amount - 1) // 2
    giver, receiver = tallies[1:1 + 2 * twos:2], tallies[2:2 + 2 * twos:2]
    margin = jnp.minimum(giver - 1, most - receiver)
    moved = jax.random.randint(jax.random.fold_in(own_key, 1), (twos,), 0, 1 << 20) % (margin + 1)
    tallies = tallies.at[1:1 + 2 * twos:2].set(giver - moved).at[2:2 + 2 * twos:2].set(receiver + moved)
    return tallies[jax.random.permutation(jax.random.fold_in(own_key, 2), amount)]


def normal_values(key, dims, width, most, cuts=(), kind=jnp.bfloat16):
    entries = jax.random.normal(key, dims, jnp.float32) * width
    if len(cuts) > 0:
        entries = levels(key, dims, cuts, -0.22, 0.18) * entries
    return jnp.clip(entries, min=-most, max=most).astype(kind)


def noise_with(own_key, dims, spread, bound, cuts, heavy, kind=jnp.bfloat16):
    values = spread * jax.random.normal(own_key, dims, jnp.float32)
    if cuts:
        values = values * levels(own_key, dims, cuts, -0.22, 0.18)
    return jnp.clip(with_spikes(values, jax.random.fold_in(own_key, 3), *heavy), -bound, bound).astype(kind)


def setup_inputs(seed: int = 0) -> dict:
    arg_keys = jax.random.split(jax.random.key(seed), 18)
    return {
        "hidden_in": noise_with(arg_keys[0], (TOKENS, D), 1.0, 6.0, ((0, 8),), (0, 1, 8, 2.0)),
        "norm_gain": jnp.clip(1.0 + 0.1 * jax.random.normal(arg_keys[1], (D,), jnp.float32), 0.5, 1.5),
        "z_weight": normal_values(arg_keys[2], (D, D_INNER), D ** -0.5, 0.125, ((1, 4),)),
        "x_weight": normal_values(arg_keys[3], (D, D_INNER), D ** -0.5, 0.125, ((1, 4),)),
        "bc_weight": normal_values(arg_keys[4], (D, 2 * STATE), D ** -0.5, 0.125),
        "dt_weight": normal_values(arg_keys[5], (D, HEADS), D ** -0.5, 0.125, ((1, 4),)),
        "conv_x": normal_values(arg_keys[6], (CONV, D_INNER), 0.5, 3.0, ((1, 4),), jnp.float32),
        "conv_x_bias": normal_values(arg_keys[7], (D_INNER,), 0.5, 3.0, ((0, 4),), jnp.float32),
        "conv_bc": normal_values(arg_keys[8], (CONV, 2 * STATE), 0.5, 3.0, (), jnp.float32),
        "conv_bc_bias": normal_values(arg_keys[9], (2 * STATE,), 0.5, 3.0, (), jnp.float32),
        "dt_bias": jnp.clip(-7.0 + 3.5 * jax.random.uniform(arg_keys[10], (HEADS,), jnp.float32) ** levels(arg_keys[10], (HEADS,), ((0, 4),), -0.2, 0.2), -7.0, -3.5),
        "a_log": jnp.clip(2.1 * jax.random.uniform(arg_keys[11], (HEADS,), jnp.float32) ** levels(arg_keys[11], (HEADS,), ((0, 4),), -0.2, 0.2), 0.0, 2.1),
        "d_skip": draw_d_skip(jax.random.fold_in(arg_keys[17], 71), 0),
        "gate_gain": jnp.clip(1.0 + 0.1 * jax.random.normal(arg_keys[13], (D_INNER,), jnp.float32), 0.5, 1.5),
        "out_weight": normal_values(arg_keys[14], (D_INNER, D), D_INNER ** -0.5, 0.09375, ((0, 4),)),
        "cotangent": noise_with(arg_keys[15], (TOKENS, D), 1.0, 6.0, ((0, 8),), (0, 1, 8, 2.0)),
        "segment_ids": jnp.searchsorted(jnp.cumsum(ragged_sizes(arg_keys[16], TOKENS // (SEQ_LEN // 4), TOKENS, SEQ_LEN // 2, 1)), jnp.arange(TOKENS), side="right").astype(jnp.int32),
    }


epsilon = 1e-05

@jax.custom_vjp
def low(v):
    return lax.optimization_barrier(v.astype(jnp.bfloat16)).astype(jnp.float32)

@jax.custom_vjp
def low_back(v):
    return v

def low_keep(v):
    return (low(v), None)

def low_pass(kept, grad):
    return (grad,)

def back_keep(v):
    return (v, None)

def back_low(kept, grad):
    return (low(grad),)
low.defvjp(low_keep, low_pass)
low_back.defvjp(back_keep, back_low)

def dot_high(left, right):
    return jnp.dot(left, right, precision=lax.Precision.HIGHEST, preferred_element_type=jnp.float32)

def causal_conv(values, kernel_taps, shift_bias, segment_ids, seq_len):
    length = values.shape[0]
    position = jnp.arange(length, dtype=jnp.int32) % seq_len
    result = shift_bias[None, :] + kernel_taps[0][None, :] * values
    for offset in range(1, kernel_taps.shape[0]):
        shifted = jnp.concatenate([jnp.zeros((offset, values.shape[1]), values.dtype), values[:-offset]], 0)
        shifted_ids = jnp.concatenate([jnp.full((offset,), -1, jnp.int32), segment_ids[:-offset]], 0)
        usable = (position >= offset) & (shifted_ids == segment_ids)
        result = result + jnp.where(usable[:, None], shifted, 0.0) * kernel_taps[offset][None, :]
    return result

def block_scan(inputs_x, steps_dt, rates, b_rows, c_rows, segment_ids, seq_len):
    length, head_count, head_width = inputs_x.shape
    states_n = b_rows.shape[1]
    blocks = length // GROUP
    per_sequence = seq_len // GROUP
    decays = steps_dt * rates[None, :]

    def to_blocks(source):
        return source.reshape((blocks, GROUP) + source.shape[1:])

    def advance(carried, pieces):
        memory, last_id = carried
        block_x, block_dt, block_decay, block_b, block_c, block_ids, number = pieces
        is_fresh = number % per_sequence == 0
        running = jnp.cumsum(block_decay, axis=0)
        across = running.T
        gap_matrix = across[:, :, None] - across[:, None, :]
        lower_mask = jnp.arange(GROUP)[:, None] >= jnp.arange(GROUP)[None, :]
        linked = (lower_mask & (block_ids[:, None] == block_ids[None, :]))[None]
        factors = jnp.where(linked, jnp.exp(jnp.where(linked, gap_matrix, 0.0)), 0.0)
        scores = jnp.dot(block_c, block_b.T, precision=lax.Precision.HIGHEST)
        weighted = scores[None] * factors * block_dt.T[:, None, :]
        inside = jnp.einsum('hts,shp->thp', weighted, block_x, precision=lax.Precision.HIGHEST)
        reading = jnp.logical_and(block_ids == last_id, jnp.logical_not(is_fresh))
        reach = jnp.exp(running) * jnp.where(reading, 1.0, 0.0)[:, None]
        outside = jnp.einsum('tn,hnp->thp', block_c, memory, precision=lax.Precision.HIGHEST) * reach[:, :, None]
        final_id = block_ids[-1]
        keeping = jnp.where(jnp.logical_and(final_id == last_id, jnp.logical_not(is_fresh)), 1.0, 0.0)
        tail_weights = jnp.exp(running[-1][None, :] - running) * block_dt * jnp.where(block_ids == final_id, 1.0, 0.0)[:, None]
        memory = keeping * jnp.exp(running[-1])[:, None, None] * memory + jnp.einsum('sn,shp->hnp', block_b, tail_weights[:, :, None] * block_x, precision=lax.Precision.HIGHEST)
        return ((memory, final_id), inside + outside)
    initial = (jnp.zeros((head_count, states_n, head_width), inputs_x.dtype), jnp.array(-1, jnp.int32))
    numbers = jnp.arange(blocks, dtype=jnp.int32)
    final_carry, outputs = lax.scan(jax.checkpoint(advance), initial, (to_blocks(inputs_x), to_blocks(steps_dt), to_blocks(decays), to_blocks(b_rows), to_blocks(c_rows), to_blocks(segment_ids), numbers))
    return outputs.reshape(length, head_count, head_width)

def mixer_core(segment_ids, seq_len, x_pre, bc_pre, dt_pre, z_pre, conv_x, conv_x_bias, conv_bc, conv_bc_bias, dt_bias, a_log, d_skip):
    length = x_pre.shape[0]
    head_count = dt_pre.shape[1]
    x_conv = jax.nn.silu(causal_conv(x_pre, conv_x, conv_x_bias, segment_ids, seq_len))
    bc_conv = jax.nn.silu(causal_conv(bc_pre, conv_bc, conv_bc_bias, segment_ids, seq_len))
    states_n = bc_conv.shape[1] // 2
    step_sizes = jax.nn.softplus(dt_pre + dt_bias[None, :])
    per_head = x_conv.reshape(length, head_count, -1)
    scanned = block_scan(per_head, step_sizes, -jnp.exp(a_log), bc_conv[:, :states_n], bc_conv[:, states_n:], segment_ids, seq_len)
    scanned = scanned + d_skip[None, :, None] * per_head
    return scanned.reshape(length, -1) * jax.nn.silu(z_pre)

def layer_block(inputs, segment_ids, params):
    norm_gain, z_weight, x_weight, bc_weight, dt_weight, conv_x, conv_x_bias, conv_bc, conv_bc_bias, dt_bias, a_log, d_skip, gate_gain, out_weight = params
    rms_inv = lax.rsqrt(lax.optimization_barrier(jnp.mean(inputs * inputs, -1, keepdims=True)) + epsilon)
    normed = low(inputs * rms_inv * norm_gain)
    z_pre = low_back(dot_high(normed, z_weight))
    x_pre = low_back(dot_high(normed, x_weight))
    bc_pre = low_back(dot_high(normed, bc_weight))
    dt_pre = low_back(dot_high(normed, dt_weight))
    gated = mixer_core(segment_ids, SEQ_LEN, x_pre, bc_pre, dt_pre, z_pre, conv_x, conv_x_bias, conv_bc, conv_bc_bias, dt_bias, a_log, d_skip)
    scale = lax.rsqrt(lax.optimization_barrier(jnp.sum(gated * gated, -1, keepdims=True)) / D_INNER + epsilon)
    unit = low(gated * gate_gain)
    proj = low_back(dot_high(unit, out_weight))
    return inputs + scale * proj

def reference(hidden_in, norm_gain, z_weight, x_weight, bc_weight, dt_weight, conv_x, conv_x_bias, conv_bc, conv_bc_bias, dt_bias, a_log, d_skip, gate_gain, out_weight, cotangent, segment_ids):
    params = tuple((entry.astype(jnp.float32) for entry in (norm_gain, z_weight, x_weight, bc_weight, dt_weight, conv_x, conv_x_bias, conv_bc, conv_bc_bias, dt_bias, a_log, d_skip, gate_gain, out_weight)))
    inputs = hidden_in.astype(jnp.float32).reshape(-1, SEQ_LEN, D)
    seq_ids = segment_ids.reshape(-1, SEQ_LEN)

    def whole(inputs_all, weights):

        def one_sequence(carried, pieces):
            return (carried, layer_block(pieces[0], pieces[1], weights))
        final_carry, rows = lax.scan(jax.checkpoint(one_sequence), jnp.zeros((), jnp.float32), (inputs_all, seq_ids))
        return rows
    output, backward = jax.vjp(whole, inputs, params)
    input_grad, weight_grads = backward(cotangent.astype(jnp.float32).reshape(inputs.shape))
    norm_gain_grad, z_weight_grad, x_weight_grad, bc_weight_grad, dt_weight_grad, conv_x_grad, conv_x_bias_grad, conv_bc_grad, conv_bc_bias_grad, dt_bias_grad, a_log_grad, d_skip_grad, gate_gain_grad, out_weight_grad = weight_grads
    return (output.reshape(TOKENS, D), input_grad.reshape(TOKENS, D), norm_gain_grad, z_weight_grad, x_weight_grad, bc_weight_grad, dt_weight_grad, conv_x_grad, conv_x_bias_grad, conv_bc_grad, conv_bc_bias_grad, dt_bias_grad, a_log_grad, d_skip_grad, gate_gain_grad, out_weight_grad)
```

```python
from functools import partial

import jax
import jax.numpy as jnp
from jax import lax
from jax.experimental import pallas as pl
from jax.experimental.pallas import tpu as pltpu
from jax.sharding import PartitionSpec as P

D_INNER = 4096
SEQ_LEN = 1024
CHUNK = 128
HEAD = 64
STATE = 128
PAIR = 2 * HEAD

epsilon = 1e-05

bf16 = jnp.bfloat16
f32 = jnp.float32


def dot(left, right, dims=((1,), (0,))):
    return lax.dot_general(left, right, (dims, ((), ())), preferred_element_type=f32)


def dot_exact(left, right, dims=((1,), (0,))):
    return lax.dot_general(
        left, right, (dims, ((), ())), precision=lax.Precision.HIGHEST, preferred_element_type=f32
    )


def split_dot(values, ones):
    high = values.astype(bf16)
    low = (values - high.astype(f32)).astype(bf16)
    return dot(high, ones) + dot(low, ones)


def sigmoid(v):
    return 1.0 / (1.0 + jnp.exp(-v))


def softplus(v):
    return jnp.maximum(v, 0.0) + jnp.log(1.0 + jnp.exp(-jnp.abs(v)))


PASSES = {q: 3 for q in ("scores", "inside", "outside", "state", "d_weight", "du_tail", "d_b", "d_c", "d_state", "d_scores")}
STATE_TYPE = f32


def two_parts(values):
    high = values.astype(bf16)
    return high, (values - high.astype(f32)).astype(bf16)


def mm(kind, left, right, dims=((1,), (0,))):
    if PASSES.get(kind, 1) == 1:
        return dot(left.astype(bf16), right.astype(bf16), dims)
    left_high, left_low = two_parts(left)
    right_high, right_low = two_parts(right)
    return (
        dot(left_high, right_high, dims)
        + dot(left_high, right_low, dims)
        + dot(left_low, right_high, dims)
    )


def seen(kind, values):
    return values.astype(bf16).astype(f32) if PASSES.get(kind, 1) == 1 else values


def conv_rows(padded, lanes, taps, aux):
    result = taps[4:5] + taps[0:1] * padded[pl.ds(8, CHUNK), lanes]
    for offset in range(1, 4):
        shifted = padded[pl.ds(8 - offset, CHUNK), lanes] * aux[:, offset - 1 : offset]
        result = result + shifted * taps[offset : offset + 1]
    return result


def chunk_terms(dt_ref, aux, head_ref, spread_ref):
    row = lax.broadcasted_iota(jnp.int32, (CHUNK, CHUNK), 0)
    col = lax.broadcasted_iota(jnp.int32, (CHUNK, CHUNK), 1)
    lower = jnp.where(row >= col, 1.0, 0.0)
    upper = jnp.where(row <= col, 1.0, 0.0)
    raw = dt_ref[...] + head_ref[0:1, :]
    step = softplus(raw)
    decay = step * head_ref[1:2, :]
    running = dot_exact(lower, decay)
    running_t = dot_exact(decay, upper, ((0,), (0,)))
    last = running[CHUNK - 1 : CHUNK, :]
    reach = jnp.exp(running) * aux[:, 6:7]
    tail = jnp.exp(last - running) * aux[:, 7:8]
    kept = jnp.exp(last) * aux[CHUNK - 1 : CHUNK, 8:9]
    spread = spread_ref[...]
    return (
        raw,
        step,
        decay,
        running,
        running_t,
        upper,
        split_dot(step, spread),
        split_dot(reach, spread),
        split_dot(tail, spread),
        split_dot(jnp.broadcast_to(kept, (8, kept.shape[1])), spread)[0:1],
    )


def pair_masks():
    lane = lax.broadcasted_iota(jnp.int32, (1, PAIR), 1)
    return jnp.where(lane < HEAD, 1.0, 0.0), jnp.where(lane < HEAD, 0.0, 1.0)


def forward_kernel(
    x_ref, x_before, z_ref, bc_ref, bc_before, dt_ref, aux_ref, ids_ref,
    chan_ref, taps_bc_ref, head_ref, spread_ref, start_ref,
    y_ref, unit_ref, square_ref, states_ref, final_ref,
    x_pad, bc_pad, memory, step_s, reach_s, tail_s,
):
    @pl.when(pl.program_id(0) == 0)
    def _():
        memory[...] = start_ref[...]
        x_pad[0:8, :] = x_before[...]
        bc_pad[0:8, :] = bc_before[...]

    @pl.when(pl.program_id(0) > 0)
    def _():
        x_pad[0:8, :] = x_pad[CHUNK:, :]
        bc_pad[0:8, :] = bc_pad[CHUNK:, :]

    aux = aux_ref[...]
    x_pad[8:, :] = x_ref[...]
    bc_pad[8:, :] = bc_ref[...]
    pre_bc = conv_rows(bc_pad, slice(None), taps_bc_ref[...], aux)
    bc = pre_bc * sigmoid(pre_bc)
    b_rows, c_rows = bc[:, :STATE], bc[:, STATE:]
    _, _, _, running, running_t, _, step_e, reach_e, tail_e, kept_e = chunk_terms(
        dt_ref, aux, head_ref, spread_ref
    )
    step_s[...] = step_e
    reach_s[...] = reach_e
    tail_s[...] = tail_e
    row = lax.broadcasted_iota(jnp.int32, (CHUNK, CHUNK), 0)
    col = lax.broadcasted_iota(jnp.int32, (CHUNK, CHUNK), 1)
    linked = (row >= col) & (aux[:, 9:10] == ids_ref[...])
    scores = jnp.where(linked, mm("scores", c_rows, b_rows, ((1,), (1,))), 0.0)
    first, second = pair_masks()
    squares = jnp.zeros((CHUNK, 1), f32)
    for pair in range(x_ref.shape[1] // PAIR):
        lanes = slice(pair * PAIR, (pair + 1) * PAIR)
        chan = chan_ref[:, lanes]
        pre = conv_rows(x_pad, lanes, chan, aux)
        x_conv = pre * sigmoid(pre)
        u = step_s[:, lanes] * x_conv
        old = memory[:, lanes]
        states_ref[0, :, lanes] = old.astype(states_ref.dtype)
        weighted = []
        for h in (2 * pair, 2 * pair + 1):
            gap = jnp.minimum(running[:, h : h + 1] - running_t[h : h + 1, :], 0.0)
            weighted.append(scores * jnp.exp(gap))
        y = mm(
            "inside", jnp.concatenate(weighted, 1), jnp.concatenate([u * first, u * second], 0)
        ) + mm("outside", c_rows, old) * reach_s[:, lanes]
        memory[:, lanes] = kept_e[:, lanes] * old + mm(
            "state", b_rows, tail_s[:, lanes] * u, ((0,), (0,))
        )
        y_ref[:, lanes] = y
        z = z_ref[:, lanes]
        gated = (y + chan[5:6] * x_conv) * (z * sigmoid(z))
        unit_ref[:, lanes] = (gated * chan[6:7]).astype(bf16)
        squares = squares + jnp.sum(gated * gated, 1, keepdims=True)
    square_ref[...] = squares
    final_ref[...] = memory[...]


def backward_kernel(
    x_ref, x_before, z_ref, bc_ref, bc_before, dt_ref, aux_ref, ids_ref,
    chan_ref, taps_bc_ref, head_ref, spread_ref,
    x_within, bc_within, gather_ref, y_ref, state_ref, next_ref, d_unit_ref, coef_ref,
    d_memory_in, dconv_in, dconv_bc_in, g_chan_in, g_bc_in, g_head_in,
    dz_ref, dx_ref, dbc_ref, ddt_ref,
    d_memory, dconv_ref, dconv_bc_ref, g_chan_ref, g_bc_ref, g_head_ref,
    x_pad, bc_pad, step_s, reach_s, tail_s, dconv_pad, dconv_bc_pad, step_grad_s, run_grad_s, later,
):
    heads = head_ref.shape[1]
    index, count = pl.program_id(0), pl.num_programs(0)

    @pl.when(index == 0)
    def _():
        d_memory[...] = d_memory_in[...]
        dconv_pad[0:8, :] = dconv_in[...]
        dconv_bc_pad[0:8, :] = dconv_bc_in[...]
        g_chan_ref[...] = g_chan_in[...]
        g_bc_ref[...] = g_bc_in[...]
        g_head_ref[...] = g_head_in[...]
        later[...] = next_ref[0]

    @pl.when(index == count - 1)
    def _():
        x_pad[0:8, :] = x_before[...]
        bc_pad[0:8, :] = bc_before[...]

    @pl.when(index < count - 1)
    def _():
        x_pad[0:8, :] = x_within[...]
        bc_pad[0:8, :] = bc_within[...]

    aux = aux_ref[...]
    x_pad[8:, :] = x_ref[...]
    bc_pad[8:, :] = bc_ref[...]
    dconv_pad[CHUNK:, :] = dconv_pad[0:8, :]
    dconv_bc_pad[CHUNK:, :] = dconv_bc_pad[0:8, :]
    taps_bc = taps_bc_ref[...]
    pre_bc = conv_rows(bc_pad, slice(None), taps_bc, aux)
    sig_bc = sigmoid(pre_bc)
    bc = pre_bc * sig_bc
    b_rows, c_rows = bc[:, :STATE], bc[:, STATE:]
    raw, step, decay, running, running_t, upper, step_e, reach_e, tail_e, kept_e = chunk_terms(
        dt_ref, aux, head_ref, spread_ref
    )
    step_s[...] = step_e
    reach_s[...] = reach_e
    tail_s[...] = tail_e
    row = lax.broadcasted_iota(jnp.int32, (CHUNK, CHUNK), 0)
    col = lax.broadcasted_iota(jnp.int32, (CHUNK, CHUNK), 1)
    linked = (row <= col) & (aux[:, 9:10] == ids_ref[...])
    scores_t = jnp.where(linked, mm("scores", b_rows, c_rows, ((1,), (1,))), 0.0)
    first, second = pair_masks()
    coef = coef_ref[...]
    d_scores_t = jnp.zeros((CHUNK, CHUNK), f32)
    d_b = jnp.zeros((CHUNK, STATE), f32)
    d_c = jnp.zeros((CHUNK, STATE), f32)
    ends = jnp.zeros((8, heads), f32)
    for pair in range(x_ref.shape[1] // PAIR):
        lanes = slice(pair * PAIR, (pair + 1) * PAIR)
        chan = chan_ref[:, lanes]
        pre = conv_rows(x_pad, lanes, chan, aux)
        sig = sigmoid(pre)
        x_conv = pre * sig
        u = step_s[:, lanes] * x_conv
        z = z_ref[:, lanes]
        sig_z = sigmoid(z)
        silu_z = z * sig_z
        y = y_ref[:, lanes]
        scanned = y + chan[5:6] * x_conv
        gated = scanned * silu_z
        d_unit = d_unit_ref[:, lanes]
        d_gated = d_unit * chan[6:7] - coef * gated
        dz_ref[:, lanes] = (d_gated * scanned * (sig_z + silu_z * (1.0 - sig_z))).astype(bf16)
        dy = d_gated * silu_z
        stacked = jnp.concatenate([dy * first, dy * second], 0)
        d_mem = d_memory[:, lanes]
        state = state_ref[0, :, lanes]
        decays, weighted = [], []
        for h in (2 * pair, 2 * pair + 1):
            gap = jnp.minimum(running_t[h : h + 1, :] - running[:, h : h + 1], 0.0)
            decays.append(jnp.exp(gap))
            weighted.append(scores_t * decays[-1])
        d_weight = mm("d_weight", u, stacked, ((1,), (1,)))
        d_scores_t = d_scores_t + d_weight[:, :CHUNK] * decays[0] + d_weight[:, CHUNK:] * decays[1]
        tail = tail_s[:, lanes]
        du = mm("inside", jnp.concatenate(weighted, 1), stacked) + mm("du_tail", b_rows, d_mem) * tail
        d_b = d_b + mm("d_b", tail * u, d_mem, ((1,), (1,)))
        reached = reach_s[:, lanes] * dy
        d_c = d_c + mm("d_c", reached, state, ((1,), (1,)))
        end = jnp.sum(d_mem * later[:, lanes].astype(f32), 0, keepdims=True)
        later[:, lanes] = state
        d_memory[:, lanes] = kept_e[:, lanes] * d_mem + mm("d_state", c_rows, reached, ((0,), (0,)))
        gather = gather_ref[lanes, :]
        ends = ends + split_dot(jnp.broadcast_to(end, (8, PAIR)), gather)
        run_part = split_dot(seen("inside", dy) * y - seen("inside", u) * du, gather)
        step_part = split_dot(x_conv * du, gather)
        if pair == 0:
            run_grad_s[...] = run_part
            step_grad_s[...] = step_part
        else:
            run_grad_s[...] += run_part
            step_grad_s[...] += step_part
        d_conv = (chan[5:6] * dy + step_s[:, lanes] * du) * (sig + x_conv * (1.0 - sig))
        dconv_pad[0:CHUNK, lanes] = d_conv
        d_pre = chan[0:1] * d_conv
        g_chan_ref[0:1, lanes] += jnp.sum(d_conv * x_ref[:, lanes], 0, keepdims=True)
        for offset in range(1, 4):
            ahead = dconv_pad[pl.ds(offset, CHUNK), lanes] * aux[:, 2 + offset : 3 + offset]
            d_pre = d_pre + chan[offset : offset + 1] * ahead
            behind = x_pad[pl.ds(8 - offset, CHUNK), lanes] * aux[:, offset - 1 : offset]
            g_chan_ref[offset : offset + 1, lanes] += jnp.sum(d_conv * behind, 0, keepdims=True)
        dx_ref[:, lanes] = d_pre.astype(bf16)
        g_chan_ref[4:5, lanes] += jnp.sum(d_conv, 0, keepdims=True)
        g_chan_ref[5:6, lanes] += jnp.sum(dy * x_conv, 0, keepdims=True)
        g_chan_ref[6:7, lanes] += jnp.sum(d_unit * gated, 0, keepdims=True)

    d_decay = dot_exact(upper, run_grad_s[...]) + ends[0:1]
    d_step = step_grad_s[...] + head_ref[1:2, :] * d_decay
    d_raw = d_step * sigmoid(raw)
    ddt_ref[...] = d_raw.astype(bf16)
    g_head_ref[0:1, :] += jnp.sum(d_raw, 0, keepdims=True)
    g_head_ref[1:2, :] += jnp.sum(d_decay * decay, 0, keepdims=True)

    d_scores_t = jnp.where(linked, d_scores_t, 0.0)
    d_b = d_b + mm("d_scores", d_scores_t, c_rows)
    d_c = d_c + mm("d_scores", d_scores_t, b_rows, ((0,), (0,)))
    d_conv = jnp.concatenate([d_b, d_c], 1) * (sig_bc + pre_bc * sig_bc * (1.0 - sig_bc))
    dconv_bc_pad[0:CHUNK, :] = d_conv
    d_pre = taps_bc[0:1] * d_conv
    g_bc_ref[0:1, :] += jnp.sum(d_conv * bc_ref[...], 0, keepdims=True)
    for offset in range(1, 4):
        ahead = dconv_bc_pad[pl.ds(offset, CHUNK), :] * aux[:, 2 + offset : 3 + offset]
        d_pre = d_pre + taps_bc[offset : offset + 1] * ahead
        behind = bc_pad[pl.ds(8 - offset, CHUNK), :] * aux[:, offset - 1 : offset]
        g_bc_ref[offset : offset + 1, :] += jnp.sum(d_conv * behind, 0, keepdims=True)
    g_bc_ref[4:5, :] += jnp.sum(d_conv, 0, keepdims=True)
    dbc_ref[...] = d_pre.astype(bf16)
    dconv_ref[...] = dconv_pad[0:8, :]
    dconv_bc_ref[...] = dconv_bc_pad[0:8, :]


def rows_spec(width, place):
    return pl.BlockSpec((CHUNK, width), lambda i: (place(i), 0))


def within_spec(width, place):
    return pl.BlockSpec((8, width), lambda i: (jnp.maximum(place(i) * (CHUNK // 8) - 1, 0), 0))


def last_rows_spec(array):
    last = array.shape[0] // 8 - 1
    return pl.BlockSpec((8, array.shape[1]), lambda i: (last, 0))


def whole_spec(shape):
    return pl.BlockSpec(shape, lambda i: (0,) * len(shape))


def sequence_specs(segment, place, first_chunk):
    x, x_before, _, _, bc_before, dt = segment[:6]
    inner, heads = x.shape[1], dt.shape[1]
    return [
        rows_spec(inner, place),
        last_rows_spec(x_before),
        rows_spec(inner, place),
        rows_spec(2 * STATE, place),
        last_rows_spec(bc_before),
        rows_spec(heads, place),
        rows_spec(16, lambda i: place(i) + first_chunk),
        pl.BlockSpec((1, CHUNK), lambda i: (0, place(i) + first_chunk)),
        whole_spec((8, inner)),
        whole_spec((8, 2 * STATE)),
        whole_spec((8, heads)),
        whole_spec((heads, inner)),
    ]


def forward_scan(segment, start, first_chunk):
    tokens, inner = segment[0].shape
    chunks = tokens // CHUNK

    def place(i):
        return i

    return pl.pallas_call(
        forward_kernel,
        grid=(chunks,),
        in_specs=sequence_specs(segment, place, first_chunk) + [whole_spec((STATE, inner))],
        out_specs=[
            rows_spec(inner, place),
            rows_spec(inner, place),
            rows_spec(1, place),
            pl.BlockSpec((1, STATE, inner), lambda i: (i, 0, 0)),
            whole_spec((STATE, inner)),
        ],
        out_shape=[
            jax.ShapeDtypeStruct((tokens, inner), f32),
            jax.ShapeDtypeStruct((tokens, inner), bf16),
            jax.ShapeDtypeStruct((tokens, 1), f32),
            jax.ShapeDtypeStruct((chunks, STATE, inner), STATE_TYPE),
            jax.ShapeDtypeStruct((STATE, inner), f32),
        ],
        scratch_shapes=[
            pltpu.VMEM((CHUNK + 8, inner), f32),
            pltpu.VMEM((CHUNK + 8, 2 * STATE), f32),
            pltpu.VMEM((STATE, inner), f32),
            pltpu.VMEM((CHUNK, inner), f32),
            pltpu.VMEM((CHUNK, inner), f32),
            pltpu.VMEM((CHUNK, inner), f32),
        ],
        compiler_params=pltpu.CompilerParams(vmem_limit_bytes=32 << 20),
        cost_estimate=pl.CostEstimate(
            flops=tokens * inner * 2000, bytes_accessed=tokens * inner * 18, transcendentals=0
        ),
        name="forward_scan",
    )(*segment, start)


def backward_scan(segment, first_chunk, gather, y, states, next_states, d_unit, coef, carried):
    tokens, inner = segment[0].shape
    heads = segment[5].shape[1]
    chunks = tokens // CHUNK

    def place(i):
        return chunks - 1 - i

    carried_specs = [whole_spec(array.shape) for array in carried]
    return pl.pallas_call(
        backward_kernel,
        grid=(chunks,),
        in_specs=sequence_specs(segment, place, first_chunk)
        + [
            within_spec(inner, place),
            within_spec(2 * STATE, place),
            whole_spec((inner, heads)),
            rows_spec(inner, place),
            pl.BlockSpec((1, STATE, inner), lambda i: (place(i), 0, 0)),
            pl.BlockSpec((1, STATE, inner), lambda i: (0, 0, 0)),
            rows_spec(inner, place),
            rows_spec(1, place),
        ]
        + carried_specs,
        out_specs=[
            rows_spec(inner, place),
            rows_spec(inner, place),
            rows_spec(2 * STATE, place),
            rows_spec(heads, place),
        ]
        + carried_specs,
        out_shape=[
            jax.ShapeDtypeStruct((tokens, inner), bf16),
            jax.ShapeDtypeStruct((tokens, inner), bf16),
            jax.ShapeDtypeStruct((tokens, 2 * STATE), bf16),
            jax.ShapeDtypeStruct((tokens, heads), bf16),
        ]
        + [jax.ShapeDtypeStruct(array.shape, f32) for array in carried],
        scratch_shapes=[
            pltpu.VMEM((CHUNK + 8, inner), f32),
            pltpu.VMEM((CHUNK + 8, 2 * STATE), f32),
            pltpu.VMEM((CHUNK, inner), f32),
            pltpu.VMEM((CHUNK, inner), f32),
            pltpu.VMEM((CHUNK, inner), f32),
            pltpu.VMEM((CHUNK + 8, inner), f32),
            pltpu.VMEM((CHUNK + 8, 2 * STATE), f32),
            pltpu.VMEM((CHUNK, heads), f32),
            pltpu.VMEM((CHUNK, heads), f32),
            pltpu.VMEM((STATE, inner), STATE_TYPE),
        ],
        compiler_params=pltpu.CompilerParams(vmem_limit_bytes=32 << 20),
        cost_estimate=pl.CostEstimate(
            flops=tokens * inner * 4000, bytes_accessed=tokens * inner * 26, transcendentals=0
        ),
        name="backward_scan",
    )(*segment, segment[0], segment[3], gather, y, states, next_states, d_unit, coef, *carried)


def backward_start(inner, heads):
    return [
        jnp.zeros(shape, f32)
        for shape in [(STATE, inner), (8, inner), (8, 2 * STATE), (8, inner), (8, 2 * STATE), (8, heads)]
    ]


def token_masks(segment_ids):
    length = segment_ids.shape[0]
    token = jnp.arange(length, dtype=jnp.int32)
    position = token % SEQ_LEN
    ids = segment_ids
    padded = jnp.concatenate([jnp.full((3,), -1, jnp.int32), ids, jnp.full((3,), -1, jnp.int32)])
    columns = []
    for offset in range(1, 4):
        columns.append((position >= offset) & (padded[3 - offset : 3 - offset + length] == ids))
    for offset in range(1, 4):
        columns.append(
            (position < SEQ_LEN - offset) & (padded[3 + offset : 3 + offset + length] == ids)
        )
    by_chunk = ids.reshape(-1, CHUNK)
    final = by_chunk[:, -1:]
    previous = jnp.concatenate([jnp.full((1, 1), -1, jnp.int32), final[:-1]], 0)
    start = jnp.arange(by_chunk.shape[0], dtype=jnp.int32)[:, None] * CHUNK
    previous = jnp.where(start % SEQ_LEN == 0, -1, previous)
    columns.append((by_chunk == previous).reshape(-1))
    columns.append((by_chunk == final).reshape(-1))
    columns.append(jnp.broadcast_to(final == previous, by_chunk.shape).reshape(-1))
    columns.append(ids)
    columns = columns + [jnp.zeros((length,), f32)] * (16 - len(columns))
    return jnp.stack([column.astype(f32) for column in columns], 1)


def contract_rows(left, right):
    return dot(left, right, ((0,), (0,)))


def contract_cols(left, right):
    return dot(left, right, ((1,), (1,)))


INWARD = [(0, 1), (3, 2)]
ACROSS = [(1, 2), (2, 1)]
OUTWARD = [(1, 0), (2, 3)]


class LineSum:
    def __init__(self, chains):
        me = lax.axis_index("tensor")
        self.outer = (me == 0) | (me == 3)
        self.waiting = []
        self.chains = [[None, None, None] for _ in range(chains)]
        self.sent = [[None, None, None] for _ in range(chains)]
        self.names = [[None, None, None] for _ in range(chains)]
        self.next = 0
        self.results = {}

    def add(self, name, piece):
        self.waiting.append((name, piece))

    def busy(self):
        return bool(self.waiting) or any(part is not None for chain in self.chains for part in chain)

    def turn(self, carried=()):
        chain = self.next
        self.next = (chain + 1) % len(self.chains)
        held, sent, names = self.chains[chain], self.sent[chain], self.names[chain]
        name, piece = self.waiting.pop(0) if self.waiting else (None, None)
        tied = lax.optimization_barrier((tuple(sent), piece, tuple(carried)))
        sent, piece, carried = tied
        inward = None if held[0] is None else held[0] + sent[0]
        across = None if held[1] is None else held[1] + sent[1]
        if held[2] is not None:
            self.results[names[2]] = jnp.where(self.outer, sent[2], held[2])
        self.chains[chain] = [piece, inward, across]
        self.names[chain] = [name, names[0], names[1]]
        self.sent[chain] = [
            None if part is None else lax.ppermute(part, "tensor", route)
            for part, route in zip(self.chains[chain], (INWARD, ACROSS, OUTWARD))
        ]
        return carried


SEGMENT = 256
PIECE = 128
CHAINS = 2


def shards(
    tensor_size,
    hidden_in,
    norm_gain,
    z_weight,
    x_weight,
    bc_weight,
    dt_weight,
    conv_x,
    conv_x_bias,
    conv_bc,
    conv_bc_bias,
    dt_bias,
    a_log,
    d_skip,
    gate_gain,
    out_weight,
    cotangent,
    segment_ids,
):
    tokens, width = hidden_in.shape
    heads = dt_bias.shape[0]
    inner = heads * HEAD
    count = tokens // SEGMENT
    chunks = SEGMENT // CHUNK
    line = LineSum(CHAINS)

    rate = -jnp.exp(a_log)
    zero_row = jnp.zeros((1, inner), f32)
    chan = jnp.concatenate(
        [conv_x, conv_x_bias[None], jnp.repeat(d_skip, HEAD)[None], gate_gain[None], zero_row], 0
    )
    taps_bc = jnp.concatenate([conv_bc, conv_bc_bias[None], jnp.zeros((3, 2 * STATE), f32)], 0)
    head_rows = jnp.concatenate([dt_bias[None], rate[None], jnp.zeros((6, heads), f32)], 0)
    owner = jnp.arange(inner, dtype=jnp.int32) // HEAD
    spread = (jnp.arange(heads, dtype=jnp.int32)[:, None] == owner[None, :]).astype(bf16)
    gather = (owner[:, None] == jnp.arange(heads, dtype=jnp.int32)[None, :]).astype(bf16)
    shared = (
        token_masks(segment_ids), segment_ids.astype(f32)[None], chan, taps_bc, head_rows, spread,
    )

    def rows(array, index):
        return lax.slice_in_dim(array, index * SEGMENT, (index + 1) * SEGMENT, axis=0)

    def split(array):
        return [array[at : at + PIECE] for at in range(0, SEGMENT, PIECE)]

    memory = jnp.zeros((STATE, inner), f32)
    segments, normed, hats, rms, ys, units, states, stats = [], [], [], [], [], [], [], []
    for index in range(count):
        hidden = rows(hidden_in, index)
        if index:
            memory, hidden = line.turn((memory, hidden))
        base = hidden.astype(f32)
        rms.append(lax.rsqrt(jnp.mean(base * base, -1, keepdims=True) + epsilon))
        normed.append((base * rms[-1] * norm_gain[None, :]).astype(bf16))
        x_pre = dot(normed[-1], x_weight)
        bc_pre = dot(normed[-1], bc_weight)
        z_pre = dot(normed[-1], z_weight)
        dt_pre = dot(normed[-1], dt_weight)
        before = segments[-1] if segments else (x_pre, None, None, bc_pre)
        segments.append((x_pre, before[0], z_pre, bc_pre, before[3], dt_pre) + shared)
        y, unit, squares, state, memory = forward_scan(segments[-1], memory, index * chunks)
        proj = dot(unit, out_weight)
        for number, piece in enumerate(split(proj)):
            line.add(("out", index * SEGMENT + number * PIECE), piece)
        share = jnp.sum(rows(cotangent, index).astype(f32) * proj, -1)
        stats.append(jnp.concatenate([squares.T, share[None]], 0))
        ys.append(y)
        units.append(unit)
        states.append(state)

    (local,) = line.turn((jnp.concatenate(stats, 1),))
    total = lax.psum(local, "tensor")
    (total,) = line.turn((total,))
    scale = lax.rsqrt(total[0] / D_INNER + epsilon)[:, None]
    d_scale = total[1][:, None]
    coef = d_scale * scale * scale * scale / D_INNER
    d_proj = (scale * cotangent.astype(f32)).astype(bf16)

    carried = backward_start(inner, heads)
    grads = [None] * count
    norm_grad = jnp.zeros((width,), f32)
    for index in reversed(range(count)):
        d_unit = contract_cols(rows(d_proj, index), out_weight)
        outs = backward_scan(
            segments[index], index * chunks, gather, ys[index], states[index],
            states[min(index + 1, count - 1)], d_unit, rows(coef, index), carried,
        )
        d_z, d_x, d_bc, d_dt = grads[index] = outs[:4]
        carried = outs[4:]
        part = (
            contract_cols(d_z, z_weight)
            + contract_cols(d_x, x_weight)
            + contract_cols(d_dt, dt_weight)
            + contract_cols(d_bc, bc_weight)
        )
        base = rows(hidden_in, index).astype(f32)
        norm_grad = norm_grad + jnp.sum(part * (base * rms[index]), 0)
        for number, piece in reversed(list(enumerate(split(part)))):
            line.add(("in", index * SEGMENT + number * PIECE), piece)
        *carried, norm_grad = line.turn(tuple(carried) + (norm_grad,))

    normed_all = jnp.concatenate(normed, 0)
    unit_all = jnp.concatenate(units, 0)
    d_z, d_x, d_bc, d_dt = [jnp.concatenate([g[k] for g in grads], 0) for k in range(4)]
    d_rest = jnp.concatenate([d_bc, d_dt], 1)
    rest_share = lax.psum_scatter(
        contract_rows(normed_all, d_rest), "dp", scatter_dimension=0, tiled=True
    )
    out_share = lax.psum_scatter(
        contract_rows(unit_all, d_proj), "dp", scatter_dimension=1, tiled=True
    )
    z_share = lax.psum_scatter(contract_rows(normed_all, d_z), "dp", scatter_dimension=0, tiled=True)
    x_share = lax.psum_scatter(contract_rows(normed_all, d_x), "dp", scatter_dimension=0, tiled=True)
    norm_grad, g_chan, g_bc, g_head = lax.psum((norm_grad,) + tuple(carried[3:]), "dp")

    bc_part = rest_share[:, : 2 * STATE]
    extra = jnp.concatenate([norm_grad, g_bc.reshape(-1), bc_part.reshape(-1)])
    extra_rows = -(-extra.shape[0] // (8 * width)) * 8
    extra = jnp.pad(extra, (0, extra_rows * width - extra.shape[0])).reshape(extra_rows, width)
    line.add(("extra", 0), extra)

    output = jnp.zeros((tokens, width), f32)
    input_grad = jnp.zeros((tokens, width), f32)
    done = 0
    while line.busy():
        line.turn()
    for (kind, at), value in line.results.items():
        if kind == "extra":
            flat = value.reshape(-1)
            norm_gain_grad = flat[:width]
            g_bc = flat[width : width + g_bc.size].reshape(g_bc.shape)
            begin = width + g_bc.size
            bc_share = flat[begin : begin + bc_part.size].reshape(bc_part.shape)
            continue
        base = hidden_in[at : at + PIECE].astype(f32)
        if kind == "out":
            result = base + scale[at : at + PIECE] * value
            output = lax.dynamic_update_slice(output, result, (at, 0))
        else:
            cot = cotangent[at : at + PIECE].astype(f32)
            inverse = rms[at // SEGMENT][at % SEGMENT : at % SEGMENT + PIECE]
            hat = base * inverse
            d_hat = value * norm_gain[None, :]
            result = cot + inverse * (d_hat - hat * jnp.mean(d_hat * hat, -1, keepdims=True))
            input_grad = lax.dynamic_update_slice(input_grad, result, (at, 0))
    return (
        output,
        input_grad,
        norm_gain_grad,
        z_share,
        x_share,
        bc_share,
        rest_share[:, 2 * STATE :],
        g_chan[:4],
        g_chan[4],
        g_bc[:4],
        g_bc[4],
        g_head[0],
        g_head[1],
        jnp.sum(g_chan[5].reshape(heads, HEAD), 1),
        g_chan[6],
        out_share,
    )


def solution(mesh):
    placed = (
        P("dp", None),
        P(),
        P(None, "tensor"),
        P(None, "tensor"),
        P(),
        P(None, "tensor"),
        P(None, "tensor"),
        P("tensor"),
        P(),
        P(),
        P("tensor"),
        P("tensor"),
        P("tensor"),
        P("tensor"),
        P("tensor", None),
        P("dp", None),
        P("dp"),
    )
    return jax.shard_map(
        partial(shards, mesh.shape["tensor"]),
        mesh=mesh,
        in_specs=placed,
        out_specs=(
            P("dp", None),
            P("dp", None),
            P(),
            P("dp", "tensor"),
            P("dp", "tensor"),
            P("dp", None),
            P("dp", "tensor"),
            P(None, "tensor"),
            P("tensor"),
            P(),
            P(),
            P("tensor"),
            P("tensor"),
            P("tensor"),
            P("tensor"),
            P("tensor", "dp"),
        ),
        check_vma=False,
    )
```

```python
from functools import partial

import jax
import jax.numpy as jnp
from jax import lax
from jax.experimental import pallas as pl
from jax.experimental.pallas import tpu as pltpu
from jax.sharding import PartitionSpec as P

D_INNER = 4096
SEQ_LEN = 1024
CHUNK = 128
HEAD = 64
STATE = 128
PAIR = 2 * HEAD
REST = 3 * STATE

epsilon = 1e-05

bf16 = jnp.bfloat16
f32 = jnp.float32


def dot(left, right, dims=((1,), (0,))):
    return lax.dot_general(left, right, (dims, ((), ())), preferred_element_type=f32)


def dot_exact(left, right, dims=((1,), (0,))):
    return lax.dot_general(
        left, right, (dims, ((), ())), precision=lax.Precision.HIGHEST, preferred_element_type=f32
    )


def split_dot(values, ones):
    high = values.astype(bf16)
    low = (values - high.astype(f32)).astype(bf16)
    return dot(high, ones) + dot(low, ones)


def sigmoid(v):
    return 1.0 / (1.0 + jnp.exp(-v))


def softplus(v):
    return jnp.maximum(v, 0.0) + jnp.log(1.0 + jnp.exp(-jnp.abs(v)))


PASSES = {q: 3 for q in ("scores", "inside", "outside", "state", "d_weight", "du_tail", "d_b", "d_c", "d_state", "d_scores")}
STATE_TYPE = f32


def two_parts(values):
    high = values.astype(bf16)
    return high, (values - high.astype(f32)).astype(bf16)


def mm(kind, left, right, dims=((1,), (0,))):
    if PASSES.get(kind, 1) == 1:
        return dot(left.astype(bf16), right.astype(bf16), dims)
    left_high, left_low = two_parts(left)
    right_high, right_low = two_parts(right)
    return (
        dot(left_high, right_high, dims)
        + dot(left_high, right_low, dims)
        + dot(left_low, right_high, dims)
    )


def seen(kind, values):
    return values.astype(bf16).astype(f32) if PASSES.get(kind, 1) == 1 else values


def conv_rows(padded, lanes, taps, aux):
    result = taps[4:5] + taps[0:1] * padded[pl.ds(8, CHUNK), lanes]
    for offset in range(1, 4):
        shifted = padded[pl.ds(8 - offset, CHUNK), lanes] * aux[:, offset - 1 : offset]
        result = result + shifted * taps[offset : offset + 1]
    return result


def chunk_terms(dt, aux, head_ref, spread_ref):
    row = lax.broadcasted_iota(jnp.int32, (CHUNK, CHUNK), 0)
    col = lax.broadcasted_iota(jnp.int32, (CHUNK, CHUNK), 1)
    lower = jnp.where(row >= col, 1.0, 0.0)
    upper = jnp.where(row <= col, 1.0, 0.0)
    raw = dt + head_ref[0:1, :]
    step = softplus(raw)
    decay = step * head_ref[1:2, :]
    running = dot_exact(lower, decay)
    running_t = dot_exact(decay, upper, ((0,), (0,)))
    last = running[CHUNK - 1 : CHUNK, :]
    reach = jnp.exp(running) * aux[:, 6:7]
    tail = jnp.exp(last - running) * aux[:, 7:8]
    kept = jnp.exp(last) * aux[CHUNK - 1 : CHUNK, 8:9]
    spread = spread_ref[...]
    return (
        raw,
        step,
        decay,
        running,
        running_t,
        upper,
        split_dot(step, spread),
        split_dot(reach, spread),
        split_dot(tail, spread),
        split_dot(jnp.broadcast_to(kept, (8, kept.shape[1])), spread)[0:1],
    )


def pair_masks():
    lane = lax.broadcasted_iota(jnp.int32, (1, PAIR), 1)
    return jnp.where(lane < HEAD, 1.0, 0.0), jnp.where(lane < HEAD, 0.0, 1.0)


def forward_kernel(
    x_ref, x_before, z_ref, rest_ref, rest_before, aux_ref, ids_ref,
    chan_ref, taps_bc_ref, head_ref, spread_ref, back_ref, start_ref,
    scanned_ref, unit_ref, stats_ref, states_ref, final_ref,
    x_pad, bc_pad, memory, step_s, reach_s, tail_s,
):
    @pl.when(pl.program_id(0) == 0)
    def _():
        memory[...] = start_ref[...]
        x_pad[0:8, :] = x_before[...]
        bc_pad[0:8, :] = rest_before[:, : 2 * STATE]

    @pl.when(pl.program_id(0) > 0)
    def _():
        x_pad[0:8, :] = x_pad[CHUNK:, :]
        bc_pad[0:8, :] = bc_pad[CHUNK:, :]

    aux = aux_ref[...]
    x_pad[8:, :] = x_ref[...]
    bc_pad[8:, :] = rest_ref[:, : 2 * STATE]
    pre_bc = conv_rows(bc_pad, slice(None), taps_bc_ref[...], aux)
    bc = pre_bc * sigmoid(pre_bc)
    b_rows, c_rows = bc[:, :STATE], bc[:, STATE:]
    _, _, _, running, running_t, _, step_e, reach_e, tail_e, kept_e = chunk_terms(
        rest_ref[:, 2 * STATE : 2 * STATE + head_ref.shape[1]], aux, head_ref, spread_ref
    )
    step_s[...] = step_e
    reach_s[...] = reach_e
    tail_s[...] = tail_e
    row = lax.broadcasted_iota(jnp.int32, (CHUNK, CHUNK), 0)
    col = lax.broadcasted_iota(jnp.int32, (CHUNK, CHUNK), 1)
    linked = (row >= col) & (aux[:, 9:10] == ids_ref[...])
    scores = jnp.where(linked, mm("scores", c_rows, b_rows, ((1,), (1,))), 0.0)
    first, second = pair_masks()
    squares = jnp.zeros((CHUNK, 1), f32)
    share = jnp.zeros((CHUNK, 1), f32)
    for pair in range(x_ref.shape[1] // PAIR):
        lanes = slice(pair * PAIR, (pair + 1) * PAIR)
        chan = chan_ref[:, lanes]
        pre = conv_rows(x_pad, lanes, chan, aux)
        x_conv = pre * sigmoid(pre)
        u = step_s[:, lanes] * x_conv
        old = memory[:, lanes]
        states_ref[0, :, lanes] = old.astype(states_ref.dtype)
        weighted = []
        for h in (2 * pair, 2 * pair + 1):
            gap = jnp.minimum(running[:, h : h + 1] - running_t[h : h + 1, :], 0.0)
            weighted.append(scores * jnp.exp(gap))
        y = mm(
            "inside", jnp.concatenate(weighted, 1), jnp.concatenate([u * first, u * second], 0)
        ) + mm("outside", c_rows, old) * reach_s[:, lanes]
        memory[:, lanes] = kept_e[:, lanes] * old + mm(
            "state", b_rows, tail_s[:, lanes] * u, ((0,), (0,))
        )
        scanned = y + chan[5:6] * x_conv
        scanned_ref[:, lanes] = scanned
        z = z_ref[:, lanes]
        gated = scanned * (z * sigmoid(z))
        unit = (gated * chan[6:7]).astype(bf16)
        unit_ref[:, lanes] = unit
        squares = squares + jnp.sum(gated * gated, 1, keepdims=True)
        share = share + jnp.sum(unit.astype(f32) * back_ref[:, lanes], 1, keepdims=True)
    stats_ref[:, 0:1] = squares
    stats_ref[:, 1:2] = share
    final_ref[...] = memory[...]


def backward_kernel(
    x_ref, x_before, z_ref, rest_ref, rest_before, aux_ref, ids_ref,
    chan_ref, taps_bc_ref, head_ref, spread_ref,
    x_within, rest_within, gather_ref, scanned_ref, state_ref, next_ref, back_ref, factors_ref,
    d_memory_in, dconv_in, dconv_bc_in, g_chan_in, g_bc_in, g_head_in,
    dz_ref, dx_ref, drest_ref,
    d_memory, dconv_ref, dconv_bc_ref, g_chan_ref, g_bc_ref, g_head_ref,
    x_pad, bc_pad, step_s, reach_s, tail_s, dconv_pad, dconv_bc_pad, step_grad_s, run_grad_s, later,
):
    heads = head_ref.shape[1]
    index, count = pl.program_id(0), pl.num_programs(0)

    @pl.when(index == 0)
    def _():
        d_memory[...] = d_memory_in[...]
        dconv_pad[0:8, :] = dconv_in[...]
        dconv_bc_pad[0:8, :] = dconv_bc_in[...]
        g_chan_ref[...] = g_chan_in[...]
        g_bc_ref[...] = g_bc_in[...]
        g_head_ref[...] = g_head_in[...]
        later[...] = next_ref[0]

    @pl.when(index == count - 1)
    def _():
        x_pad[0:8, :] = x_before[...]
        bc_pad[0:8, :] = rest_before[:, : 2 * STATE]

    @pl.when(index < count - 1)
    def _():
        x_pad[0:8, :] = x_within[...]
        bc_pad[0:8, :] = rest_within[:, : 2 * STATE]

    aux = aux_ref[...]
    x_pad[8:, :] = x_ref[...]
    bc_pad[8:, :] = rest_ref[:, : 2 * STATE]
    dconv_pad[CHUNK:, :] = dconv_pad[0:8, :]
    dconv_bc_pad[CHUNK:, :] = dconv_bc_pad[0:8, :]
    taps_bc = taps_bc_ref[...]
    pre_bc = conv_rows(bc_pad, slice(None), taps_bc, aux)
    sig_bc = sigmoid(pre_bc)
    bc = pre_bc * sig_bc
    b_rows, c_rows = bc[:, :STATE], bc[:, STATE:]
    raw, step, decay, running, running_t, upper, step_e, reach_e, tail_e, kept_e = chunk_terms(
        rest_ref[:, 2 * STATE : 2 * STATE + head_ref.shape[1]], aux, head_ref, spread_ref
    )
    step_s[...] = step_e
    reach_s[...] = reach_e
    tail_s[...] = tail_e
    row = lax.broadcasted_iota(jnp.int32, (CHUNK, CHUNK), 0)
    col = lax.broadcasted_iota(jnp.int32, (CHUNK, CHUNK), 1)
    linked = (row <= col) & (aux[:, 9:10] == ids_ref[...])
    scores_t = jnp.where(linked, mm("scores", b_rows, c_rows, ((1,), (1,))), 0.0)
    first, second = pair_masks()
    scale = factors_ref[:, 0:1]
    coef = factors_ref[:, 1:2]
    d_scores_t = jnp.zeros((CHUNK, CHUNK), f32)
    d_b = jnp.zeros((CHUNK, STATE), f32)
    d_c = jnp.zeros((CHUNK, STATE), f32)
    ends = jnp.zeros((8, heads), f32)
    for pair in range(x_ref.shape[1] // PAIR):
        lanes = slice(pair * PAIR, (pair + 1) * PAIR)
        chan = chan_ref[:, lanes]
        pre = conv_rows(x_pad, lanes, chan, aux)
        sig = sigmoid(pre)
        x_conv = pre * sig
        u = step_s[:, lanes] * x_conv
        z = z_ref[:, lanes]
        sig_z = sigmoid(z)
        silu_z = z * sig_z
        scanned = scanned_ref[:, lanes]
        y = scanned - chan[5:6] * x_conv
        gated = scanned * silu_z
        d_unit = scale * back_ref[:, lanes]
        d_gated = d_unit * chan[6:7] - coef * gated
        dz_ref[:, lanes] = (d_gated * scanned * (sig_z + silu_z * (1.0 - sig_z))).astype(bf16)
        dy = d_gated * silu_z
        stacked = jnp.concatenate([dy * first, dy * second], 0)
        d_mem = d_memory[:, lanes]
        state = state_ref[0, :, lanes]
        decays, weighted = [], []
        for h in (2 * pair, 2 * pair + 1):
            gap = jnp.minimum(running_t[h : h + 1, :] - running[:, h : h + 1], 0.0)
            decays.append(jnp.exp(gap))
            weighted.append(scores_t * decays[-1])
        d_weight = mm("d_weight", u, stacked, ((1,), (1,)))
        d_scores_t = d_scores_t + d_weight[:, :CHUNK] * decays[0] + d_weight[:, CHUNK:] * decays[1]
        tail = tail_s[:, lanes]
        du = mm("inside", jnp.concatenate(weighted, 1), stacked) + mm("du_tail", b_rows, d_mem) * tail
        d_b = d_b + mm("d_b", tail * u, d_mem, ((1,), (1,)))
        reached = reach_s[:, lanes] * dy
        d_c = d_c + mm("d_c", reached, state, ((1,), (1,)))
        end = jnp.sum(d_mem * later[:, lanes].astype(f32), 0, keepdims=True)
        later[:, lanes] = state
        d_memory[:, lanes] = kept_e[:, lanes] * d_mem + mm("d_state", c_rows, reached, ((0,), (0,)))
        gather = gather_ref[lanes, :]
        ends = ends + split_dot(jnp.broadcast_to(end, (8, PAIR)), gather)
        run_part = split_dot(seen("inside", dy) * y - seen("inside", u) * du, gather)
        step_part = split_dot(x_conv * du, gather)
        if pair == 0:
            run_grad_s[...] = run_part
            step_grad_s[...] = step_part
        else:
            run_grad_s[...] += run_part
            step_grad_s[...] += step_part
        d_conv = (chan[5:6] * dy + step_s[:, lanes] * du) * (sig + x_conv * (1.0 - sig))
        dconv_pad[0:CHUNK, lanes] = d_conv
        d_pre = chan[0:1] * d_conv
        g_chan_ref[0:1, lanes] += jnp.sum(d_conv * x_ref[:, lanes], 0, keepdims=True)
        for offset in range(1, 4):
            ahead = dconv_pad[pl.ds(offset, CHUNK), lanes] * aux[:, 2 + offset : 3 + offset]
            d_pre = d_pre + chan[offset : offset + 1] * ahead
            behind = x_pad[pl.ds(8 - offset, CHUNK), lanes] * aux[:, offset - 1 : offset]
            g_chan_ref[offset : offset + 1, lanes] += jnp.sum(d_conv * behind, 0, keepdims=True)
        dx_ref[:, lanes] = d_pre.astype(bf16)
        g_chan_ref[4:5, lanes] += jnp.sum(d_conv, 0, keepdims=True)
        g_chan_ref[5:6, lanes] += jnp.sum(dy * x_conv, 0, keepdims=True)
        g_chan_ref[6:7, lanes] += jnp.sum(d_unit * gated, 0, keepdims=True)

    d_decay = dot_exact(upper, run_grad_s[...]) + ends[0:1]
    d_step = step_grad_s[...] + head_ref[1:2, :] * d_decay
    d_raw = d_step * sigmoid(raw)
    drest_ref[:, 2 * STATE :] = jnp.zeros((CHUNK, REST - 2 * STATE), bf16)
    drest_ref[:, 2 * STATE : 2 * STATE + heads] = d_raw.astype(bf16)
    g_head_ref[0:1, :] += jnp.sum(d_raw, 0, keepdims=True)
    g_head_ref[1:2, :] += jnp.sum(d_decay * decay, 0, keepdims=True)

    d_scores_t = jnp.where(linked, d_scores_t, 0.0)
    d_b = d_b + mm("d_scores", d_scores_t, c_rows)
    d_c = d_c + mm("d_scores", d_scores_t, b_rows, ((0,), (0,)))
    d_conv = jnp.concatenate([d_b, d_c], 1) * (sig_bc + pre_bc * sig_bc * (1.0 - sig_bc))
    dconv_bc_pad[0:CHUNK, :] = d_conv
    d_pre = taps_bc[0:1] * d_conv
    g_bc_ref[0:1, :] += jnp.sum(d_conv * rest_ref[:, : 2 * STATE], 0, keepdims=True)
    for offset in range(1, 4):
        ahead = dconv_bc_pad[pl.ds(offset, CHUNK), :] * aux[:, 2 + offset : 3 + offset]
        d_pre = d_pre + taps_bc[offset : offset + 1] * ahead
        behind = bc_pad[pl.ds(8 - offset, CHUNK), :] * aux[:, offset - 1 : offset]
        g_bc_ref[offset : offset + 1, :] += jnp.sum(d_conv * behind, 0, keepdims=True)
    g_bc_ref[4:5, :] += jnp.sum(d_conv, 0, keepdims=True)
    drest_ref[:, : 2 * STATE] = d_pre.astype(bf16)
    dconv_ref[...] = dconv_pad[0:8, :]
    dconv_bc_ref[...] = dconv_bc_pad[0:8, :]


def rows_spec(width, place):
    return pl.BlockSpec((CHUNK, width), lambda i: (place(i), 0))


def within_spec(width, place):
    return pl.BlockSpec((8, width), lambda i: (jnp.maximum(place(i) * (CHUNK // 8) - 1, 0), 0))


def fixed_rows_spec(width, block):
    return pl.BlockSpec((8, width), lambda i: (block, 0))


def whole_spec(shape):
    return pl.BlockSpec(shape, lambda i: (0,) * len(shape))


def sequence_specs(segment, place, first_chunk, before):
    inner, heads = segment[0].shape[1], segment[-1].shape[0]
    return [
        rows_spec(inner, place),
        fixed_rows_spec(inner, before),
        rows_spec(inner, place),
        rows_spec(REST, place),
        fixed_rows_spec(REST, before),
        rows_spec(16, lambda i: place(i) + first_chunk),
        pl.BlockSpec((1, CHUNK), lambda i: (0, place(i) + first_chunk)),
        whole_spec((8, inner)),
        whole_spec((8, 2 * STATE)),
        whole_spec((8, heads)),
        whole_spec((heads, inner)),
    ]


def forward_scan(segment, back, start, first_chunk):
    tokens, inner = segment[0].shape
    chunks = tokens // CHUNK

    def place(i):
        return i

    return pl.pallas_call(
        forward_kernel,
        grid=(chunks,),
        in_specs=sequence_specs(segment, place, first_chunk, segment[1].shape[0] // 8 - 1)
        + [rows_spec(inner, place), whole_spec((STATE, inner))],
        out_specs=[
            rows_spec(inner, place),
            rows_spec(inner, place),
            rows_spec(2, place),
            pl.BlockSpec((1, STATE, inner), lambda i: (i, 0, 0)),
            whole_spec((STATE, inner)),
        ],
        out_shape=[
            jax.ShapeDtypeStruct((tokens, inner), f32),
            jax.ShapeDtypeStruct((tokens, inner), bf16),
            jax.ShapeDtypeStruct((tokens, 2), f32),
            jax.ShapeDtypeStruct((chunks, STATE, inner), STATE_TYPE),
            jax.ShapeDtypeStruct((STATE, inner), f32),
        ],
        scratch_shapes=[
            pltpu.VMEM((CHUNK + 8, inner), f32),
            pltpu.VMEM((CHUNK + 8, 2 * STATE), f32),
            pltpu.VMEM((STATE, inner), f32),
            pltpu.VMEM((CHUNK, inner), f32),
            pltpu.VMEM((CHUNK, inner), f32),
            pltpu.VMEM((CHUNK, inner), f32),
        ],
        compiler_params=pltpu.CompilerParams(vmem_limit_bytes=24 << 20),
        cost_estimate=pl.CostEstimate(
            flops=0, bytes_accessed=0, transcendentals=0
        ),
        name="forward_scan",
    )(*segment, back, start)


def backward_scan(
    segment, first_chunk, offset, tokens, gather, scanned, states, next_states, next_at, back, factors,
    carried,
):
    inner, heads = segment[0].shape[1], segment[-1].shape[0]
    chunks = tokens // CHUNK
    x_before, rest_before, before = segment[1], segment[4], segment[1].shape[0] // 8 - 1
    if offset:
        x_before, rest_before, before = segment[0], segment[3], offset * (CHUNK // 8) - 1
    segment = (segment[0], x_before, segment[2], segment[3], rest_before) + tuple(segment[5:])

    def place(i):
        return offset + chunks - 1 - i

    def own(i):
        return chunks - 1 - i

    carried_specs = [whole_spec(array.shape) for array in carried]
    return pl.pallas_call(
        backward_kernel,
        grid=(chunks,),
        in_specs=sequence_specs(segment, place, first_chunk, before)
        + [
            within_spec(inner, place),
            within_spec(REST, place),
            whole_spec((inner, heads)),
            rows_spec(inner, place),
            pl.BlockSpec((1, STATE, inner), lambda i: (place(i), 0, 0)),
            pl.BlockSpec((1, STATE, inner), lambda i: (next_at, 0, 0)),
            rows_spec(inner, place),
            rows_spec(3, lambda i: place(i) + first_chunk),
        ]
        + carried_specs,
        out_specs=[rows_spec(inner, own), rows_spec(inner, own), rows_spec(REST, own)]
        + carried_specs,
        out_shape=[
            jax.ShapeDtypeStruct((tokens, inner), bf16),
            jax.ShapeDtypeStruct((tokens, inner), bf16),
            jax.ShapeDtypeStruct((tokens, REST), bf16),
        ]
        + [jax.ShapeDtypeStruct(array.shape, f32) for array in carried],
        scratch_shapes=[
            pltpu.VMEM((CHUNK + 8, inner), f32),
            pltpu.VMEM((CHUNK + 8, 2 * STATE), f32),
            pltpu.VMEM((CHUNK, inner), f32),
            pltpu.VMEM((CHUNK, inner), f32),
            pltpu.VMEM((CHUNK, inner), f32),
            pltpu.VMEM((CHUNK + 8, inner), f32),
            pltpu.VMEM((CHUNK + 8, 2 * STATE), f32),
            pltpu.VMEM((CHUNK, heads), f32),
            pltpu.VMEM((CHUNK, heads), f32),
            pltpu.VMEM((STATE, inner), STATE_TYPE),
        ],
        compiler_params=pltpu.CompilerParams(vmem_limit_bytes=56 << 20),
        cost_estimate=pl.CostEstimate(
            flops=0, bytes_accessed=0, transcendentals=0
        ),
        name="backward_scan",
    )(
        *segment, segment[0], segment[3], gather, scanned, states, next_states, back, factors, *carried
    )


def backward_start(inner, heads):
    return [
        jnp.zeros(shape, f32)
        for shape in [(STATE, inner), (8, inner), (8, 2 * STATE), (8, inner), (8, 2 * STATE), (8, heads)]
    ]


def normed_kernel(
    d_z, d_x, d_rest, z_weight, x_weight, rest_weight, hidden, factors, part_ref, norm_grad_ref
):
    part = (
        dot(d_z[...], z_weight[...], ((1,), (1,)))
        + dot(d_x[...], x_weight[...], ((1,), (1,)))
        + dot(d_rest[...], rest_weight[...], ((1,), (1,)))
    )
    part_ref[...] = part
    hat = hidden[...].astype(f32) * factors[:, 2:3]
    norm_grad_ref[...] = jnp.broadcast_to(jnp.sum(part * hat, 0, keepdims=True), norm_grad_ref.shape)


def normed_gradient(d_z, d_x, d_rest, z_weight, x_weight, rest_weight, hidden, factors, begin):
    tokens, inner = d_z.shape
    width = hidden.shape[1]
    tile = 256
    return pl.pallas_call(
        normed_kernel,
        grid=(width // tile,),
        in_specs=[
            whole_spec((tokens, inner)),
            whole_spec((tokens, inner)),
            whole_spec((tokens, REST)),
            pl.BlockSpec((tile, inner), lambda i: (i, 0)),
            pl.BlockSpec((tile, inner), lambda i: (i, 0)),
            pl.BlockSpec((tile, REST), lambda i: (i, 0)),
            pl.BlockSpec((tokens, tile), lambda i: (begin // tokens, i)),
            pl.BlockSpec((tokens, 3), lambda i: (begin // tokens, 0)),
        ],
        out_specs=[
            pl.BlockSpec((tokens, tile), lambda i: (0, i)),
            pl.BlockSpec((8, tile), lambda i: (0, i)),
        ],
        out_shape=[
            jax.ShapeDtypeStruct((tokens, width), f32),
            jax.ShapeDtypeStruct((8, width), f32),
        ],
        compiler_params=pltpu.CompilerParams(vmem_limit_bytes=56 << 20),
        cost_estimate=pl.CostEstimate(flops=0, bytes_accessed=0, transcendentals=0),
        name="normed_gradient",
    )(d_z, d_x, d_rest, z_weight, x_weight, rest_weight, hidden, factors)


def token_masks(segment_ids):
    length = segment_ids.shape[0]
    token = jnp.arange(length, dtype=jnp.int32)
    position = token % SEQ_LEN
    ids = segment_ids
    padded = jnp.concatenate([jnp.full((3,), -1, jnp.int32), ids, jnp.full((3,), -1, jnp.int32)])
    columns = []
    for offset in range(1, 4):
        columns.append((position >= offset) & (padded[3 - offset : 3 - offset + length] == ids))
    for offset in range(1, 4):
        columns.append(
            (position < SEQ_LEN - offset) & (padded[3 + offset : 3 + offset + length] == ids)
        )
    by_chunk = ids.reshape(-1, CHUNK)
    final = by_chunk[:, -1:]
    previous = jnp.concatenate([jnp.full((1, 1), -1, jnp.int32), final[:-1]], 0)
    start = jnp.arange(by_chunk.shape[0], dtype=jnp.int32)[:, None] * CHUNK
    previous = jnp.where(start % SEQ_LEN == 0, -1, previous)
    columns.append((by_chunk == previous).reshape(-1))
    columns.append((by_chunk == final).reshape(-1))
    columns.append(jnp.broadcast_to(final == previous, by_chunk.shape).reshape(-1))
    columns.append(ids)
    columns = columns + [jnp.zeros((length,), f32)] * (16 - len(columns))
    return jnp.stack([column.astype(f32) for column in columns], 1)


def contract_rows(left, right):
    return dot(left, right, ((0,), (0,)))


def contract_cols(left, right):
    return dot(left, right, ((1,), (1,)))


INWARD = [(0, 1), (3, 2)]
ACROSS = [(1, 2), (2, 1)]
OUTWARD = [(1, 0), (2, 3)]


class LineSum:
    def __init__(self):
        me = lax.axis_index("tensor")
        self.outer = (me == 0) | (me == 3)
        self.waiting, self.flying, self.landed, self.unfinished = [], [], [], []
        self.finish = None

    def add(self, name, piece):
        self.waiting.append((name, piece))

    def busy(self):
        return bool(self.waiting or self.flying or self.landed)

    def sums(self, pieces):
        return [(name, jnp.where(self.outer, got, own)) for name, own, got in pieces]

    def start_finishing(self, finish, after):
        names = [name for name, _, _ in self.unfinished]
        parts, after = lax.optimization_barrier(([part[1:] for part in self.unfinished], after))
        self.unfinished = [(name,) + tuple(part) for name, part in zip(names, parts)]
        self.finish = finish
        return after

    def arrive(self, got):
        for (kind, name, own, inside), moved in zip(self.flying, got):
            if kind == "both":
                self.landed.append(("in",) + inside + (moved,))
                self.landed.append(("out", name, own, moved))
            else:
                self.landed.append((kind, name, own, moved))
        self.flying = []

    def turn(self, carried=()):
        changed = {}
        if self.finish is not None:
            changed = self.finish(self.sums(self.unfinished[:4]))
            self.unfinished = self.unfinished[4:]
        got, changed, carried = lax.optimization_barrier(
            ([flight[1] for flight in self.flying], changed, tuple(carried))
        )
        if changed:
            self.finish.whole.update(changed)
        self.flying = [flight[0] for flight in self.flying]
        self.arrive(got)
        send = []
        fresh = self.waiting.pop(0) if self.waiting else None
        beside = self.waiting.pop(0) if self.waiting and self.waiting[0][0][0] == "extra" else None
        for kind, name, own, got in self.landed:
            if kind == "in":
                send.append(("across", name, own + got, None))
            elif kind == "out":
                self.unfinished.append((name, own, got))
            elif fresh is not None and fresh[1].shape == own.shape:
                joint = jnp.where(self.outer, fresh[1], own + got)
                send.insert(0, ("both", name, joint, fresh))
                fresh = None
            else:
                send.append(("out", name, own + got, None))
        for piece in (beside, fresh):
            if piece is not None:
                send.insert(0, ("in", piece[0], piece[1], None))
        self.landed = []
        ready, carried = lax.optimization_barrier(([part[2] for part in send], tuple(carried)))
        routes = {"both": INWARD + OUTWARD, "in": INWARD, "across": ACROSS, "out": OUTWARD}
        for (kind, name, _, inside), part in zip(send, ready):
            moved = lax.ppermute(part, "tensor", routes[kind])
            self.flying.append(((kind, name, part, inside), moved))
        return carried


class Finish:
    def __init__(self, base, cot, norm_gain, rms, scale):
        self.base, self.cot, self.norm_gain, self.rms, self.scale = base, cot, norm_gain, rms, scale
        self.whole = {kind: jnp.zeros(base.shape, f32) for kind in ("out", "in")}

    def __call__(self, pieces):
        changed = []
        for (kind, at, size), value in pieces:
            if kind == "extra":
                self.whole[kind] = value
            else:
                base = self.base[at : at + size].astype(f32)
                if kind == "out":
                    result = base + self.scale[at : at + size] * value
                else:
                    inverse = self.rms[at : at + size]
                    hat = base * inverse
                    d_hat = value * self.norm_gain[None, :]
                    result = self.cot[at : at + size].astype(f32) + inverse * (
                        d_hat - hat * jnp.mean(d_hat * hat, -1, keepdims=True)
                    )
                self.whole[kind] = lax.dynamic_update_slice(self.whole[kind], result, (at, 0))
            changed.append(kind)
        return {kind: self.whole[kind] for kind in sorted(set(changed))}


SEGMENT = 256
PIECES = (256,)
LAST_PIECES = (128, 128)


def shards(
    tensor_size,
    hidden_in,
    norm_gain,
    z_weight,
    x_weight,
    bc_weight,
    dt_weight,
    conv_x,
    conv_x_bias,
    conv_bc,
    conv_bc_bias,
    dt_bias,
    a_log,
    d_skip,
    gate_gain,
    out_weight,
    cotangent,
    segment_ids,
):
    tokens, width = hidden_in.shape
    heads = dt_bias.shape[0]
    inner = heads * HEAD
    count = tokens // SEGMENT
    chunks = SEGMENT // CHUNK
    line = LineSum()

    rate = -jnp.exp(a_log)
    zero_row = jnp.zeros((1, inner), f32)
    chan = jnp.concatenate(
        [conv_x, conv_x_bias[None], jnp.repeat(d_skip, HEAD)[None], gate_gain[None], zero_row], 0
    )
    taps_bc = jnp.concatenate([conv_bc, conv_bc_bias[None], jnp.zeros((3, 2 * STATE), f32)], 0)
    head_rows = jnp.concatenate([dt_bias[None], rate[None], jnp.zeros((6, heads), f32)], 0)
    owner = jnp.arange(inner, dtype=jnp.int32) // HEAD
    spread = (jnp.arange(heads, dtype=jnp.int32)[:, None] == owner[None, :]).astype(bf16)
    gather = (owner[:, None] == jnp.arange(heads, dtype=jnp.int32)[None, :]).astype(bf16)
    rest_weight = jnp.concatenate(
        [bc_weight, dt_weight, jnp.zeros((width, REST - 2 * STATE - heads), bf16)], 1
    )
    shared = (
        token_masks(segment_ids), segment_ids.astype(f32)[None], chan, taps_bc, head_rows, spread,
    )

    def pieces(kind, begin, array, sizes):
        at = 0
        for size in sizes:
            line.add((kind, begin + at, size), rows(array, at, at + size))
            at += size

    def rows(array, begin, end):
        return lax.slice_in_dim(array, begin, end, axis=0)

    memory = jnp.zeros((STATE, inner), f32)
    bounds = [(at, at + SEGMENT) for at in range(0, tokens, SEGMENT)]
    count = len(bounds)
    backs = []
    gain = norm_gain
    segments, normed, rms, scans, units, states, stats = [], [], [], [], [], [], []
    for index, (begin, end) in enumerate(bounds):
        base = rows(hidden_in, begin, end).astype(f32)
        rms.append(lax.rsqrt(jnp.mean(base * base, -1, keepdims=True) + epsilon))
        normed.append((base * rms[-1] * gain[None, :]).astype(bf16))
        x_pre = dot(normed[-1], x_weight)
        rest_pre = dot(normed[-1], rest_weight)
        z_pre = dot(normed[-1], z_weight)
        backs.append(contract_cols(rows(cotangent, begin, end), out_weight))
        before = segments[-1] if segments else (x_pre, None, None, rest_pre)
        segments.append((x_pre, before[0], z_pre, rest_pre, before[3]) + shared)
        scanned, unit, stat, state, memory = forward_scan(
            segments[-1], backs[-1], memory, begin // CHUNK
        )
        piece = dot(unit, out_weight)
        pieces("out", begin, piece, PIECES)
        if index in (0, 2):
            memory, gain = line.turn((memory, gain))
        stats.append(stat)
        scans.append(scanned)
        units.append(unit)
        states.append(state)

    rms_all = jnp.concatenate(rms, 0)
    total = lax.psum(jnp.concatenate(stats, 0), "tensor")
    (total,) = line.turn((total,))
    scale = lax.rsqrt(total[:, 0:1] / D_INNER + epsilon)
    coef = total[:, 1:2] * scale * scale * scale / D_INNER
    factors = jnp.concatenate([scale, coef, rms_all], 1)
    normed_all = jnp.concatenate(normed, 0)
    units_all = jnp.concatenate(units, 0)

    carried = backward_start(inner, heads)
    grads = []
    norm_grad = jnp.zeros((8, width), f32)
    for index in reversed(range(count)):
        begin, end = bounds[index]
        d_z, d_x, d_rest, *carried = backward_scan(
            segments[index], begin // CHUNK, 0, SEGMENT, gather, scans[index],
            states[index], states[min(index + 1, count - 1)], 0, backs[index], factors, carried,
        )
        grads.append((d_z, d_x, d_rest))
        part, share = normed_gradient(
            d_z, d_x, d_rest, z_weight, x_weight, rest_weight, hidden_in, factors, begin
        )
        norm_grad = norm_grad + share
        pieces("in", begin, part, PIECES if begin else LAST_PIECES)
        if index == count - 1:
            d_proj = (scale * cotangent.astype(f32)).astype(bf16)
            out_grad = contract_rows(units_all, d_proj)
            *carried, norm_grad, out_grad = line.turn((*carried, norm_grad, out_grad))
            out_share = lax.psum_scatter(out_grad, "dp", scatter_dimension=1, tiled=True)
        else:
            *carried, norm_grad = line.turn((*carried, norm_grad))

    d_z, d_x, d_rest = [jnp.concatenate([g[k] for g in reversed(grads)], 0) for k in range(3)]
    d_z, d_rest, out_share = lax.optimization_barrier((d_z, d_rest, out_share))
    rest_grad = contract_rows(normed_all, d_rest)
    z_grad = contract_rows(normed_all, d_z)
    rest_share = lax.psum_scatter(rest_grad, "dp", scatter_dimension=0, tiled=True)
    z_grad, d_x, rest_share, *carried = line.turn((z_grad, d_x, rest_share, *carried))
    z_share = lax.psum_scatter(z_grad, "dp", scatter_dimension=0, tiled=True)
    norm_grad, g_chan, g_bc, g_head = lax.psum((norm_grad[0], *carried[3:]), "dp")
    x_grad = contract_rows(normed_all, d_x)
    x_grad, norm_grad = line.turn((x_grad, norm_grad))
    x_grad, z_share = lax.optimization_barrier((x_grad, z_share))
    x_share = lax.psum_scatter(x_grad, "dp", scatter_dimension=0, tiled=True)

    bc_part = rest_share[:, : 2 * STATE]
    extra = jnp.concatenate([norm_grad, g_bc.reshape(-1), bc_part.reshape(-1)])
    extra_rows = -(-extra.shape[0] // (8 * width)) * 8
    extra = jnp.pad(extra, (0, extra_rows * width - extra.shape[0])).reshape(extra_rows, width)
    extra = line.start_finishing(
        Finish(hidden_in, cotangent, norm_gain, rms_all, scale), extra
    )
    line.add(("extra", 0, extra_rows), extra)

    while line.busy():
        line.turn()
    line.finish.whole.update(line.finish(line.sums(line.unfinished)))
    output, input_grad = line.finish.whole["out"], line.finish.whole["in"]
    flat = line.finish.whole["extra"].reshape(-1)
    norm_gain_grad = flat[:width]
    g_bc = flat[width : width + g_bc.size].reshape(g_bc.shape)
    begin = width + g_bc.size
    bc_share = flat[begin : begin + bc_part.size].reshape(bc_part.shape)
    return (
        output,
        input_grad,
        norm_gain_grad,
        z_share,
        x_share,
        bc_share,
        rest_share[:, 2 * STATE : 2 * STATE + heads],
        g_chan[:4],
        g_chan[4],
        g_bc[:4],
        g_bc[4],
        g_head[0],
        g_head[1],
        jnp.sum(g_chan[5].reshape(heads, HEAD), 1),
        g_chan[6],
        out_share,
    )


def solution(mesh):
    placed = (
        P("dp", None),
        P(),
        P(None, "tensor"),
        P(None, "tensor"),
        P(),
        P(None, "tensor"),
        P(None, "tensor"),
        P("tensor"),
        P(),
        P(),
        P("tensor"),
        P("tensor"),
        P("tensor"),
        P("tensor"),
        P("tensor", None),
        P("dp", None),
        P("dp"),
    )
    return jax.shard_map(
        partial(shards, mesh.shape["tensor"]),
        mesh=mesh,
        in_specs=placed,
        out_specs=(
            P("dp", None),
            P("dp", None),
            P(),
            P("dp", "tensor"),
            P("dp", "tensor"),
            P("dp", None),
            P("dp", "tensor"),
            P(None, "tensor"),
            P("tensor"),
            P(),
            P(),
            P("tensor"),
            P("tensor"),
            P("tensor"),
            P("tensor"),
            P("tensor", "dp"),
        ),
        check_vma=False,
    )
```

```python
from functools import partial

import jax
import jax.numpy as jnp
from jax import lax
from jax.experimental import pallas as pl
from jax.experimental.pallas import tpu as pltpu
from jax.sharding import PartitionSpec as P

D_INNER = 4096
SEQ_LEN = 1024
CHUNK = 128
HEAD = 64
STATE = 128
PAIR = 2 * HEAD
REST = 3 * STATE

epsilon = 1e-05

bf16 = jnp.bfloat16
f32 = jnp.float32


def dot(left, right, dims=((1,), (0,))):
    return lax.dot_general(left, right, (dims, ((), ())), preferred_element_type=f32)


def dot_exact(left, right, dims=((1,), (0,))):
    return lax.dot_general(
        left, right, (dims, ((), ())), precision=lax.Precision.HIGHEST, preferred_element_type=f32
    )


def split_dot(values, ones):
    high = values.astype(bf16)
    low = (values - high.astype(f32)).astype(bf16)
    return dot(high, ones) + dot(low, ones)


def sigmoid(v):
    return 1.0 / (1.0 + jnp.exp(-v))


def softplus(v):
    return jnp.maximum(v, 0.0) + jnp.log(1.0 + jnp.exp(-jnp.abs(v)))


PASSES = {q: 3 for q in ("scores", "inside", "outside", "state", "d_weight", "du_tail", "d_b", "d_c", "d_state", "d_scores")}
STATE_TYPE = f32


def two_parts(values):
    high = values.astype(bf16)
    return high, (values - high.astype(f32)).astype(bf16)


def mm(kind, left, right, dims=((1,), (0,))):
    if PASSES.get(kind, 1) == 1:
        return dot(left.astype(bf16), right.astype(bf16), dims)
    left_high, left_low = two_parts(left)
    right_high, right_low = two_parts(right)
    return (
        dot(left_high, right_high, dims)
        + dot(left_high, right_low, dims)
        + dot(left_low, right_high, dims)
    )


def seen(kind, values):
    return values.astype(bf16).astype(f32) if PASSES.get(kind, 1) == 1 else values


def conv_rows(padded, lanes, taps, aux):
    result = taps[4:5] + taps[0:1] * padded[pl.ds(8, CHUNK), lanes]
    for offset in range(1, 4):
        shifted = padded[pl.ds(8 - offset, CHUNK), lanes] * aux[:, offset - 1 : offset]
        result = result + shifted * taps[offset : offset + 1]
    return result


def chunk_terms(dt, aux, head_ref, spread_ref):
    row = lax.broadcasted_iota(jnp.int32, (CHUNK, CHUNK), 0)
    col = lax.broadcasted_iota(jnp.int32, (CHUNK, CHUNK), 1)
    lower = jnp.where(row >= col, 1.0, 0.0)
    upper = jnp.where(row <= col, 1.0, 0.0)
    raw = dt + head_ref[0:1, :]
    step = softplus(raw)
    decay = step * head_ref[1:2, :]
    running = dot_exact(lower, decay)
    running_t = dot_exact(decay, upper, ((0,), (0,)))
    last = running[CHUNK - 1 : CHUNK, :]
    reach = jnp.exp(running) * aux[:, 6:7]
    tail = jnp.exp(last - running) * aux[:, 7:8]
    kept = jnp.exp(last) * aux[CHUNK - 1 : CHUNK, 8:9]
    spread = spread_ref[...]
    return (
        raw,
        step,
        decay,
        running,
        running_t,
        upper,
        split_dot(step, spread),
        split_dot(reach, spread),
        split_dot(tail, spread),
        split_dot(jnp.broadcast_to(kept, (8, kept.shape[1])), spread)[0:1],
    )


def pair_masks():
    lane = lax.broadcasted_iota(jnp.int32, (1, PAIR), 1)
    return jnp.where(lane < HEAD, 1.0, 0.0), jnp.where(lane < HEAD, 0.0, 1.0)


def forward_kernel(
    x_ref, x_before, z_ref, rest_ref, rest_before, aux_ref, ids_ref,
    chan_ref, taps_bc_ref, head_ref, spread_ref, back_ref, start_ref,
    scanned_ref, unit_ref, stats_ref, states_ref, final_ref,
    x_pad, bc_pad, memory, step_s, reach_s, tail_s,
):
    @pl.when(pl.program_id(0) == 0)
    def _():
        memory[...] = start_ref[...]
        x_pad[0:8, :] = x_before[...]
        bc_pad[0:8, :] = rest_before[:, : 2 * STATE]

    @pl.when(pl.program_id(0) > 0)
    def _():
        x_pad[0:8, :] = x_pad[CHUNK:, :]
        bc_pad[0:8, :] = bc_pad[CHUNK:, :]

    aux = aux_ref[...]
    x_pad[8:, :] = x_ref[...]
    bc_pad[8:, :] = rest_ref[:, : 2 * STATE]
    pre_bc = conv_rows(bc_pad, slice(None), taps_bc_ref[...], aux)
    bc = pre_bc * sigmoid(pre_bc)
    b_rows, c_rows = bc[:, :STATE], bc[:, STATE:]
    _, _, _, running, running_t, _, step_e, reach_e, tail_e, kept_e = chunk_terms(
        rest_ref[:, 2 * STATE : 2 * STATE + head_ref.shape[1]], aux, head_ref, spread_ref
    )
    step_s[...] = step_e
    reach_s[...] = reach_e
    tail_s[...] = tail_e
    row = lax.broadcasted_iota(jnp.int32, (CHUNK, CHUNK), 0)
    col = lax.broadcasted_iota(jnp.int32, (CHUNK, CHUNK), 1)
    linked = (row >= col) & (aux[:, 9:10] == ids_ref[...])
    scores = jnp.where(linked, mm("scores", c_rows, b_rows, ((1,), (1,))), 0.0)
    first, second = pair_masks()
    squares = jnp.zeros((CHUNK, 1), f32)
    share = jnp.zeros((CHUNK, 1), f32)
    for pair in range(x_ref.shape[1] // PAIR):
        lanes = slice(pair * PAIR, (pair + 1) * PAIR)
        chan = chan_ref[:, lanes]
        pre = conv_rows(x_pad, lanes, chan, aux)
        x_conv = pre * sigmoid(pre)
        u = step_s[:, lanes] * x_conv
        old = memory[:, lanes]
        states_ref[0, :, lanes] = old.astype(states_ref.dtype)
        weighted = []
        for h in (2 * pair, 2 * pair + 1):
            gap = jnp.minimum(running[:, h : h + 1] - running_t[h : h + 1, :], 0.0)
            weighted.append(scores * jnp.exp(gap))
        y = mm(
            "inside", jnp.concatenate(weighted, 1), jnp.concatenate([u * first, u * second], 0)
        ) + mm("outside", c_rows, old) * reach_s[:, lanes]
        memory[:, lanes] = kept_e[:, lanes] * old + mm(
            "state", b_rows, tail_s[:, lanes] * u, ((0,), (0,))
        )
        scanned = y + chan[5:6] * x_conv
        scanned_ref[:, lanes] = scanned
        z = z_ref[:, lanes]
        gated = scanned * (z * sigmoid(z))
        unit = (gated * chan[6:7]).astype(bf16)
        unit_ref[:, lanes] = unit
        squares = squares + jnp.sum(gated * gated, 1, keepdims=True)
        share = share + jnp.sum(unit.astype(f32) * back_ref[:, lanes], 1, keepdims=True)
    stats_ref[:, 0:1] = squares
    stats_ref[:, 1:2] = share
    final_ref[...] = memory[...]


def backward_kernel(
    x_ref, x_before, z_ref, rest_ref, rest_before, aux_ref, ids_ref,
    chan_ref, taps_bc_ref, head_ref, spread_ref,
    x_within, rest_within, gather_ref, scanned_ref, state_ref, next_ref, back_ref, factors_ref,
    d_memory_in, dconv_in, dconv_bc_in, g_chan_in, g_bc_in, g_head_in,
    dz_ref, dx_ref, drest_ref,
    d_memory, dconv_ref, dconv_bc_ref, g_chan_ref, g_bc_ref, g_head_ref,
    x_pad, bc_pad, step_s, reach_s, tail_s, dconv_pad, dconv_bc_pad, step_grad_s, run_grad_s, later,
):
    heads = head_ref.shape[1]
    index, count = pl.program_id(0), pl.num_programs(0)

    @pl.when(index == 0)
    def _():
        d_memory[...] = d_memory_in[...]
        dconv_pad[0:8, :] = dconv_in[...]
        dconv_bc_pad[0:8, :] = dconv_bc_in[...]
        g_chan_ref[...] = g_chan_in[...]
        g_bc_ref[...] = g_bc_in[...]
        g_head_ref[...] = g_head_in[...]
        later[...] = next_ref[0]

    @pl.when(index == count - 1)
    def _():
        x_pad[0:8, :] = x_before[...]
        bc_pad[0:8, :] = rest_before[:, : 2 * STATE]

    @pl.when(index < count - 1)
    def _():
        x_pad[0:8, :] = x_within[...]
        bc_pad[0:8, :] = rest_within[:, : 2 * STATE]

    aux = aux_ref[...]
    x_pad[8:, :] = x_ref[...]
    bc_pad[8:, :] = rest_ref[:, : 2 * STATE]
    dconv_pad[CHUNK:, :] = dconv_pad[0:8, :]
    dconv_bc_pad[CHUNK:, :] = dconv_bc_pad[0:8, :]
    taps_bc = taps_bc_ref[...]
    pre_bc = conv_rows(bc_pad, slice(None), taps_bc, aux)
    sig_bc = sigmoid(pre_bc)
    bc = pre_bc * sig_bc
    b_rows, c_rows = bc[:, :STATE], bc[:, STATE:]
    raw, step, decay, running, running_t, upper, step_e, reach_e, tail_e, kept_e = chunk_terms(
        rest_ref[:, 2 * STATE : 2 * STATE + head_ref.shape[1]], aux, head_ref, spread_ref
    )
    step_s[...] = step_e
    reach_s[...] = reach_e
    tail_s[...] = tail_e
    row = lax.broadcasted_iota(jnp.int32, (CHUNK, CHUNK), 0)
    col = lax.broadcasted_iota(jnp.int32, (CHUNK, CHUNK), 1)
    linked = (row <= col) & (aux[:, 9:10] == ids_ref[...])
    scores_t = jnp.where(linked, mm("scores", b_rows, c_rows, ((1,), (1,))), 0.0)
    first, second = pair_masks()
    scale = factors_ref[:, 0:1]
    coef = factors_ref[:, 1:2]
    d_scores_t = jnp.zeros((CHUNK, CHUNK), f32)
    d_b = jnp.zeros((CHUNK, STATE), f32)
    d_c = jnp.zeros((CHUNK, STATE), f32)
    ends = jnp.zeros((8, heads), f32)
    for pair in range(x_ref.shape[1] // PAIR):
        lanes = slice(pair * PAIR, (pair + 1) * PAIR)
        chan = chan_ref[:, lanes]
        pre = conv_rows(x_pad, lanes, chan, aux)
        sig = sigmoid(pre)
        x_conv = pre * sig
        u = step_s[:, lanes] * x_conv
        z = z_ref[:, lanes]
        sig_z = sigmoid(z)
        silu_z = z * sig_z
        scanned = scanned_ref[:, lanes]
        y = scanned - chan[5:6] * x_conv
        gated = scanned * silu_z
        d_unit = scale * back_ref[:, lanes]
        d_gated = d_unit * chan[6:7] - coef * gated
        dz_ref[:, lanes] = (d_gated * scanned * (sig_z + silu_z * (1.0 - sig_z))).astype(bf16)
        dy = d_gated * silu_z
        stacked = jnp.concatenate([dy * first, dy * second], 0)
        d_mem = d_memory[:, lanes]
        state = state_ref[0, :, lanes]
        decays, weighted = [], []
        for h in (2 * pair, 2 * pair + 1):
            gap = jnp.minimum(running_t[h : h + 1, :] - running[:, h : h + 1], 0.0)
            decays.append(jnp.exp(gap))
            weighted.append(scores_t * decays[-1])
        d_weight = mm("d_weight", u, stacked, ((1,), (1,)))
        d_scores_t = d_scores_t + d_weight[:, :CHUNK] * decays[0] + d_weight[:, CHUNK:] * decays[1]
        tail = tail_s[:, lanes]
        du = mm("inside", jnp.concatenate(weighted, 1), stacked) + mm("du_tail", b_rows, d_mem) * tail
        d_b = d_b + mm("d_b", tail * u, d_mem, ((1,), (1,)))
        reached = reach_s[:, lanes] * dy
        d_c = d_c + mm("d_c", reached, state, ((1,), (1,)))
        end = jnp.sum(d_mem * later[:, lanes].astype(f32), 0, keepdims=True)
        later[:, lanes] = state
        d_memory[:, lanes] = kept_e[:, lanes] * d_mem + mm("d_state", c_rows, reached, ((0,), (0,)))
        gather = gather_ref[lanes, :]
        ends = ends + split_dot(jnp.broadcast_to(end, (8, PAIR)), gather)
        run_part = split_dot(seen("inside", dy) * y - seen("inside", u) * du, gather)
        step_part = split_dot(x_conv * du, gather)
        if pair == 0:
            run_grad_s[...] = run_part
            step_grad_s[...] = step_part
        else:
            run_grad_s[...] += run_part
            step_grad_s[...] += step_part
        d_conv = (chan[5:6] * dy + step_s[:, lanes] * du) * (sig + x_conv * (1.0 - sig))
        dconv_pad[0:CHUNK, lanes] = d_conv
        d_pre = chan[0:1] * d_conv
        g_chan_ref[0:1, lanes] += jnp.sum(d_conv * x_ref[:, lanes], 0, keepdims=True)
        for offset in range(1, 4):
            ahead = dconv_pad[pl.ds(offset, CHUNK), lanes] * aux[:, 2 + offset : 3 + offset]
            d_pre = d_pre + chan[offset : offset + 1] * ahead
            behind = x_pad[pl.ds(8 - offset, CHUNK), lanes] * aux[:, offset - 1 : offset]
            g_chan_ref[offset : offset + 1, lanes] += jnp.sum(d_conv * behind, 0, keepdims=True)
        dx_ref[:, lanes] = d_pre.astype(bf16)
        g_chan_ref[4:5, lanes] += jnp.sum(d_conv, 0, keepdims=True)
        g_chan_ref[5:6, lanes] += jnp.sum(dy * x_conv, 0, keepdims=True)
        g_chan_ref[6:7, lanes] += jnp.sum(d_unit * gated, 0, keepdims=True)

    d_decay = dot_exact(upper, run_grad_s[...]) + ends[0:1]
    d_step = step_grad_s[...] + head_ref[1:2, :] * d_decay
    d_raw = d_step * sigmoid(raw)
    drest_ref[:, 2 * STATE :] = jnp.zeros((CHUNK, REST - 2 * STATE), bf16)
    drest_ref[:, 2 * STATE : 2 * STATE + heads] = d_raw.astype(bf16)
    g_head_ref[0:1, :] += jnp.sum(d_raw, 0, keepdims=True)
    g_head_ref[1:2, :] += jnp.sum(d_decay * decay, 0, keepdims=True)

    d_scores_t = jnp.where(linked, d_scores_t, 0.0)
    d_b = d_b + mm("d_scores", d_scores_t, c_rows)
    d_c = d_c + mm("d_scores", d_scores_t, b_rows, ((0,), (0,)))
    d_conv = jnp.concatenate([d_b, d_c], 1) * (sig_bc + pre_bc * sig_bc * (1.0 - sig_bc))
    dconv_bc_pad[0:CHUNK, :] = d_conv
    d_pre = taps_bc[0:1] * d_conv
    g_bc_ref[0:1, :] += jnp.sum(d_conv * rest_ref[:, : 2 * STATE], 0, keepdims=True)
    for offset in range(1, 4):
        ahead = dconv_bc_pad[pl.ds(offset, CHUNK), :] * aux[:, 2 + offset : 3 + offset]
        d_pre = d_pre + taps_bc[offset : offset + 1] * ahead
        behind = bc_pad[pl.ds(8 - offset, CHUNK), :] * aux[:, offset - 1 : offset]
        g_bc_ref[offset : offset + 1, :] += jnp.sum(d_conv * behind, 0, keepdims=True)
    g_bc_ref[4:5, :] += jnp.sum(d_conv, 0, keepdims=True)
    drest_ref[:, : 2 * STATE] = d_pre.astype(bf16)
    dconv_ref[...] = dconv_pad[0:8, :]
    dconv_bc_ref[...] = dconv_bc_pad[0:8, :]


def rows_spec(width, place):
    return pl.BlockSpec((CHUNK, width), lambda i: (place(i), 0))


def within_spec(width, place):
    return pl.BlockSpec((8, width), lambda i: (jnp.maximum(place(i) * (CHUNK // 8) - 1, 0), 0))


def fixed_rows_spec(width, block):
    return pl.BlockSpec((8, width), lambda i: (block, 0))


def whole_spec(shape):
    return pl.BlockSpec(shape, lambda i: (0,) * len(shape))


def sequence_specs(segment, place, first_chunk, before):
    inner, heads = segment[0].shape[1], segment[-1].shape[0]
    return [
        rows_spec(inner, place),
        fixed_rows_spec(inner, before),
        rows_spec(inner, place),
        rows_spec(REST, place),
        fixed_rows_spec(REST, before),
        rows_spec(16, lambda i: place(i) + first_chunk),
        pl.BlockSpec((1, CHUNK), lambda i: (0, place(i) + first_chunk)),
        whole_spec((8, inner)),
        whole_spec((8, 2 * STATE)),
        whole_spec((8, heads)),
        whole_spec((heads, inner)),
    ]


def forward_scan(segment, back, start, first_chunk):
    tokens, inner = segment[0].shape
    chunks = tokens // CHUNK

    def place(i):
        return i

    return pl.pallas_call(
        forward_kernel,
        grid=(chunks,),
        in_specs=sequence_specs(segment, place, first_chunk, segment[1].shape[0] // 8 - 1)
        + [rows_spec(inner, place), whole_spec((STATE, inner))],
        out_specs=[
            rows_spec(inner, place),
            rows_spec(inner, place),
            rows_spec(2, place),
            pl.BlockSpec((1, STATE, inner), lambda i: (i, 0, 0)),
            whole_spec((STATE, inner)),
        ],
        out_shape=[
            jax.ShapeDtypeStruct((tokens, inner), f32),
            jax.ShapeDtypeStruct((tokens, inner), bf16),
            jax.ShapeDtypeStruct((tokens, 2), f32),
            jax.ShapeDtypeStruct((chunks, STATE, inner), STATE_TYPE),
            jax.ShapeDtypeStruct((STATE, inner), f32),
        ],
        scratch_shapes=[
            pltpu.VMEM((CHUNK + 8, inner), f32),
            pltpu.VMEM((CHUNK + 8, 2 * STATE), f32),
            pltpu.VMEM((STATE, inner), f32),
            pltpu.VMEM((CHUNK, inner), f32),
            pltpu.VMEM((CHUNK, inner), f32),
            pltpu.VMEM((CHUNK, inner), f32),
        ],
        compiler_params=pltpu.CompilerParams(vmem_limit_bytes=24 << 20),
        cost_estimate=pl.CostEstimate(
            flops=0, bytes_accessed=0, transcendentals=0
        ),
        name="forward_scan",
    )(*segment, back, start)


def backward_scan(
    segment, first_chunk, offset, tokens, gather, scanned, states, next_states, next_at, back, factors,
    carried,
):
    inner, heads = segment[0].shape[1], segment[-1].shape[0]
    chunks = tokens // CHUNK
    x_before, rest_before, before = segment[1], segment[4], segment[1].shape[0] // 8 - 1
    if offset:
        x_before, rest_before, before = segment[0], segment[3], offset * (CHUNK // 8) - 1
    segment = (segment[0], x_before, segment[2], segment[3], rest_before) + tuple(segment[5:])

    def place(i):
        return offset + chunks - 1 - i

    def own(i):
        return chunks - 1 - i

    carried_specs = [whole_spec(array.shape) for array in carried]
    return pl.pallas_call(
        backward_kernel,
        grid=(chunks,),
        in_specs=sequence_specs(segment, place, first_chunk, before)
        + [
            within_spec(inner, place),
            within_spec(REST, place),
            whole_spec((inner, heads)),
            rows_spec(inner, place),
            pl.BlockSpec((1, STATE, inner), lambda i: (place(i), 0, 0)),
            pl.BlockSpec((1, STATE, inner), lambda i: (next_at, 0, 0)),
            rows_spec(inner, place),
            rows_spec(3, lambda i: place(i) + first_chunk),
        ]
        + carried_specs,
        out_specs=[rows_spec(inner, own), rows_spec(inner, own), rows_spec(REST, own)]
        + carried_specs,
        out_shape=[
            jax.ShapeDtypeStruct((tokens, inner), bf16),
            jax.ShapeDtypeStruct((tokens, inner), bf16),
            jax.ShapeDtypeStruct((tokens, REST), bf16),
        ]
        + [jax.ShapeDtypeStruct(array.shape, f32) for array in carried],
        scratch_shapes=[
            pltpu.VMEM((CHUNK + 8, inner), f32),
            pltpu.VMEM((CHUNK + 8, 2 * STATE), f32),
            pltpu.VMEM((CHUNK, inner), f32),
            pltpu.VMEM((CHUNK, inner), f32),
            pltpu.VMEM((CHUNK, inner), f32),
            pltpu.VMEM((CHUNK + 8, inner), f32),
            pltpu.VMEM((CHUNK + 8, 2 * STATE), f32),
            pltpu.VMEM((CHUNK, heads), f32),
            pltpu.VMEM((CHUNK, heads), f32),
            pltpu.VMEM((STATE, inner), STATE_TYPE),
        ],
        compiler_params=pltpu.CompilerParams(vmem_limit_bytes=56 << 20),
        cost_estimate=pl.CostEstimate(
            flops=0, bytes_accessed=0, transcendentals=0
        ),
        name="backward_scan",
    )(
        *segment, segment[0], segment[3], gather, scanned, states, next_states, back, factors, *carried
    )


def backward_start(inner, heads):
    return [
        jnp.zeros(shape, f32)
        for shape in [(STATE, inner), (8, inner), (8, 2 * STATE), (8, inner), (8, 2 * STATE), (8, heads)]
    ]


def normed_kernel(
    d_z, d_x, d_rest, z_weight, x_weight, rest_weight, hidden, factors, part_ref, norm_grad_ref
):
    part = (
        dot(d_z[...], z_weight[...], ((1,), (1,)))
        + dot(d_x[...], x_weight[...], ((1,), (1,)))
        + dot(d_rest[...], rest_weight[...], ((1,), (1,)))
    )
    part_ref[...] = part
    hat = hidden[...].astype(f32) * factors[:, 2:3]
    norm_grad_ref[...] = jnp.broadcast_to(jnp.sum(part * hat, 0, keepdims=True), norm_grad_ref.shape)


def normed_gradient(d_z, d_x, d_rest, z_weight, x_weight, rest_weight, hidden, factors, begin):
    tokens, inner = d_z.shape
    width = hidden.shape[1]
    tile = 256
    return pl.pallas_call(
        normed_kernel,
        grid=(width // tile,),
        in_specs=[
            whole_spec((tokens, inner)),
            whole_spec((tokens, inner)),
            whole_spec((tokens, REST)),
            pl.BlockSpec((tile, inner), lambda i: (i, 0)),
            pl.BlockSpec((tile, inner), lambda i: (i, 0)),
            pl.BlockSpec((tile, REST), lambda i: (i, 0)),
            pl.BlockSpec((tokens, tile), lambda i: (begin // tokens, i)),
            pl.BlockSpec((tokens, 3), lambda i: (begin // tokens, 0)),
        ],
        out_specs=[
            pl.BlockSpec((tokens, tile), lambda i: (0, i)),
            pl.BlockSpec((8, tile), lambda i: (0, i)),
        ],
        out_shape=[
            jax.ShapeDtypeStruct((tokens, width), f32),
            jax.ShapeDtypeStruct((8, width), f32),
        ],
        compiler_params=pltpu.CompilerParams(vmem_limit_bytes=56 << 20),
        cost_estimate=pl.CostEstimate(flops=0, bytes_accessed=0, transcendentals=0),
        name="normed_gradient",
    )(d_z, d_x, d_rest, z_weight, x_weight, rest_weight, hidden, factors)


def token_masks(segment_ids):
    length = segment_ids.shape[0]
    token = jnp.arange(length, dtype=jnp.int32)
    position = token % SEQ_LEN
    ids = segment_ids
    padded = jnp.concatenate([jnp.full((3,), -1, jnp.int32), ids, jnp.full((3,), -1, jnp.int32)])
    columns = []
    for offset in range(1, 4):
        columns.append((position >= offset) & (padded[3 - offset : 3 - offset + length] == ids))
    for offset in range(1, 4):
        columns.append(
            (position < SEQ_LEN - offset) & (padded[3 + offset : 3 + offset + length] == ids)
        )
    by_chunk = ids.reshape(-1, CHUNK)
    final = by_chunk[:, -1:]
    previous = jnp.concatenate([jnp.full((1, 1), -1, jnp.int32), final[:-1]], 0)
    start = jnp.arange(by_chunk.shape[0], dtype=jnp.int32)[:, None] * CHUNK
    previous = jnp.where(start % SEQ_LEN == 0, -1, previous)
    columns.append((by_chunk == previous).reshape(-1))
    columns.append((by_chunk == final).reshape(-1))
    columns.append(jnp.broadcast_to(final == previous, by_chunk.shape).reshape(-1))
    columns.append(ids)
    columns = columns + [jnp.zeros((length,), f32)] * (16 - len(columns))
    return jnp.stack([column.astype(f32) for column in columns], 1)


def contract_rows(left, right):
    return dot(left, right, ((0,), (0,)))


def contract_cols(left, right):
    return dot(left, right, ((1,), (1,)))


INWARD = [(0, 1), (3, 2)]
ACROSS = [(1, 2), (2, 1)]
OUTWARD = [(1, 0), (2, 3)]


class LineSum:
    def __init__(self):
        me = lax.axis_index("tensor")
        self.outer = (me == 0) | (me == 3)
        self.waiting, self.flying, self.landed, self.unfinished = [], [], [], []
        self.finish = None

    def add(self, name, piece):
        self.waiting.append((name, piece))

    def busy(self):
        return bool(self.waiting or self.flying or self.landed)

    def sums(self, pieces):
        return [(name, jnp.where(self.outer, got, own)) for name, own, got in pieces]

    def start_finishing(self, finish, after):
        names = [name for name, _, _ in self.unfinished]
        parts, after = lax.optimization_barrier(([part[1:] for part in self.unfinished], after))
        self.unfinished = [(name,) + tuple(part) for name, part in zip(names, parts)]
        self.finish = finish
        return after

    def arrive(self, got):
        for (kind, name, own, inside), moved in zip(self.flying, got):
            if kind == "both":
                self.landed.append(("in",) + inside + (moved,))
                self.landed.append(("out", name, own, moved))
            else:
                self.landed.append((kind, name, own, moved))
        self.flying = []

    def turn(self, carried=()):
        changed = {}
        if self.finish is not None:
            changed = self.finish(self.sums(self.unfinished[:4]))
            self.unfinished = self.unfinished[4:]
        got, changed, carried = lax.optimization_barrier(
            ([flight[1] for flight in self.flying], changed, tuple(carried))
        )
        if changed:
            self.finish.whole.update(changed)
        self.flying = [flight[0] for flight in self.flying]
        self.arrive(got)
        send = []
        fresh = self.waiting.pop(0) if self.waiting else None
        beside = self.waiting.pop(0) if self.waiting and self.waiting[0][0][0] == "extra" else None
        for kind, name, own, got in self.landed:
            if kind == "in":
                send.append(("across", name, own + got, None))
            elif kind == "out":
                self.unfinished.append((name, own, got))
            elif fresh is not None and fresh[1].shape == own.shape:
                joint = jnp.where(self.outer, fresh[1], own + got)
                send.insert(0, ("both", name, joint, fresh))
                fresh = None
            else:
                send.append(("out", name, own + got, None))
        for piece in (beside, fresh):
            if piece is not None:
                send.insert(0, ("in", piece[0], piece[1], None))
        self.landed = []
        ready, carried = lax.optimization_barrier(([part[2] for part in send], tuple(carried)))
        routes = {"both": INWARD + OUTWARD, "in": INWARD, "across": ACROSS, "out": OUTWARD}
        for (kind, name, _, inside), part in zip(send, ready):
            moved = lax.ppermute(part, "tensor", routes[kind])
            self.flying.append(((kind, name, part, inside), moved))
        return carried


class Finish:
    def __init__(self, base, cot, norm_gain, rms, scale):
        self.base, self.cot, self.norm_gain, self.rms, self.scale = base, cot, norm_gain, rms, scale
        self.whole = {kind: jnp.zeros(base.shape, f32) for kind in ("out", "in")}

    def __call__(self, pieces):
        changed = []
        for (kind, at, size), value in pieces:
            if kind == "extra":
                self.whole[kind] = value
            else:
                base = self.base[at : at + size].astype(f32)
                if kind == "out":
                    result = base + self.scale[at : at + size] * value
                else:
                    inverse = self.rms[at : at + size]
                    hat = base * inverse
                    d_hat = value * self.norm_gain[None, :]
                    result = self.cot[at : at + size].astype(f32) + inverse * (
                        d_hat - hat * jnp.mean(d_hat * hat, -1, keepdims=True)
                    )
                self.whole[kind] = lax.dynamic_update_slice(self.whole[kind], result, (at, 0))
            changed.append(kind)
        return {kind: self.whole[kind] for kind in sorted(set(changed))}


SEGMENT = 256
PIECES = (256,)
LAST_PIECES = (128, 128)


def shards(
    tensor_size,
    hidden_in,
    norm_gain,
    z_weight,
    x_weight,
    bc_weight,
    dt_weight,
    conv_x,
    conv_x_bias,
    conv_bc,
    conv_bc_bias,
    dt_bias,
    a_log,
    d_skip,
    gate_gain,
    out_weight,
    cotangent,
    segment_ids,
):
    tokens, width = hidden_in.shape
    heads = dt_bias.shape[0]
    inner = heads * HEAD
    count = tokens // SEGMENT
    chunks = SEGMENT // CHUNK
    line = LineSum()

    rate = -jnp.exp(a_log)
    zero_row = jnp.zeros((1, inner), f32)
    chan = jnp.concatenate(
        [conv_x, conv_x_bias[None], jnp.repeat(d_skip, HEAD)[None], gate_gain[None], zero_row], 0
    )
    taps_bc = jnp.concatenate([conv_bc, conv_bc_bias[None], jnp.zeros((3, 2 * STATE), f32)], 0)
    head_rows = jnp.concatenate([dt_bias[None], rate[None], jnp.zeros((6, heads), f32)], 0)
    owner = jnp.arange(inner, dtype=jnp.int32) // HEAD
    spread = (jnp.arange(heads, dtype=jnp.int32)[:, None] == owner[None, :]).astype(bf16)
    gather = (owner[:, None] == jnp.arange(heads, dtype=jnp.int32)[None, :]).astype(bf16)
    rest_weight = jnp.concatenate(
        [bc_weight, dt_weight, jnp.zeros((width, REST - 2 * STATE - heads), bf16)], 1
    )
    shared = (
        token_masks(segment_ids), segment_ids.astype(f32)[None], chan, taps_bc, head_rows, spread,
    )

    def pieces(kind, begin, array, sizes):
        at = 0
        for size in sizes:
            line.add((kind, begin + at, size), rows(array, at, at + size))
            at += size

    def rows(array, begin, end):
        return lax.slice_in_dim(array, begin, end, axis=0)

    memory = jnp.zeros((STATE, inner), f32)
    bounds = [(at, at + SEGMENT) for at in range(0, tokens, SEGMENT)]
    count = len(bounds)
    backs = []
    gain = norm_gain
    segments, normed, rms, scans, units, states, stats = [], [], [], [], [], [], []
    for index, (begin, end) in enumerate(bounds):
        base = rows(hidden_in, begin, end).astype(f32)
        rms.append(lax.rsqrt(jnp.mean(base * base, -1, keepdims=True) + epsilon))
        normed.append((base * rms[-1] * gain[None, :]).astype(bf16))
        x_pre = dot(normed[-1], x_weight)
        rest_pre = dot(normed[-1], rest_weight)
        z_pre = dot(normed[-1], z_weight)
        backs.append(contract_cols(rows(cotangent, begin, end), out_weight))
        before = segments[-1] if segments else (x_pre, None, None, rest_pre)
        segments.append((x_pre, before[0], z_pre, rest_pre, before[3]) + shared)
        scanned, unit, stat, state, memory = forward_scan(
            segments[-1], backs[-1], memory, begin // CHUNK
        )
        piece = dot(unit, out_weight)
        pieces("out", begin, piece, PIECES)
        if index in (0, 2):
            memory, gain = line.turn((memory, gain))
        stats.append(stat)
        scans.append(scanned)
        units.append(unit)
        states.append(state)

    rms_all = jnp.concatenate(rms, 0)
    total = lax.psum(jnp.concatenate(stats, 0), "tensor")
    (total,) = line.turn((total,))
    scale = lax.rsqrt(total[:, 0:1] / D_INNER + epsilon)
    coef = total[:, 1:2] * scale * scale * scale / D_INNER
    factors = jnp.concatenate([scale, coef, rms_all], 1)
    normed_all = jnp.concatenate(normed, 0)
    units_all = jnp.concatenate(units, 0)

    carried = backward_start(inner, heads)
    grads = []
    norm_grad = jnp.zeros((8, width), f32)
    for index in reversed(range(count)):
        begin, end = bounds[index]
        d_z, d_x, d_rest, *carried = backward_scan(
            segments[index], begin // CHUNK, 0, SEGMENT, gather, scans[index],
            states[index], states[min(index + 1, count - 1)], 0, backs[index], factors, carried,
        )
        grads.append((d_z, d_x, d_rest))
        part, share = normed_gradient(
            d_z, d_x, d_rest, z_weight, x_weight, rest_weight, hidden_in, factors, begin
        )
        norm_grad = norm_grad + share
        pieces("in", begin, part, PIECES if begin else LAST_PIECES)
        if index == count - 1:
            d_proj = (scale * cotangent.astype(f32)).astype(bf16)
            out_grad = contract_rows(units_all, d_proj)
            *carried, norm_grad, out_grad = line.turn((*carried, norm_grad, out_grad))
            out_share = lax.psum_scatter(out_grad, "dp", scatter_dimension=1, tiled=True)
        else:
            *carried, norm_grad = line.turn((*carried, norm_grad))

    d_z, d_x, d_rest = [jnp.concatenate([g[k] for g in reversed(grads)], 0) for k in range(3)]
    d_z, d_rest, out_share = lax.optimization_barrier((d_z, d_rest, out_share))
    rest_grad = contract_rows(normed_all, d_rest)
    z_grad = contract_rows(normed_all, d_z)
    rest_share = lax.psum_scatter(rest_grad, "dp", scatter_dimension=0, tiled=True)
    z_grad, d_x, rest_share, *carried = line.turn((z_grad, d_x, rest_share, *carried))
    z_share = lax.psum_scatter(z_grad, "dp", scatter_dimension=0, tiled=True)
    norm_grad, g_chan, g_bc, g_head = lax.psum((norm_grad[0], *carried[3:]), "dp")
    bc_part = rest_share[:, : 2 * STATE]
    extra = jnp.concatenate([norm_grad, g_bc.reshape(-1), bc_part.reshape(-1)])
    extra_rows = -(-extra.shape[0] // (8 * width)) * 8
    extra = jnp.pad(extra, (0, extra_rows * width - extra.shape[0])).reshape(extra_rows, width)
    line.add(("extra", 0, extra_rows), extra)
    (d_x,) = line.turn((d_x,))
    d_x = line.start_finishing(Finish(hidden_in, cotangent, norm_gain, rms_all, scale), d_x)
    x_grad = contract_rows(normed_all, d_x)
    x_share = lax.psum_scatter(x_grad, "dp", scatter_dimension=0, tiled=True)

    while line.busy():
        line.turn()
    line.finish.whole.update(line.finish(line.sums(line.unfinished)))
    output, input_grad = line.finish.whole["out"], line.finish.whole["in"]
    flat = line.finish.whole["extra"].reshape(-1)
    norm_gain_grad = flat[:width]
    g_bc = flat[width : width + g_bc.size].reshape(g_bc.shape)
    begin = width + g_bc.size
    bc_share = flat[begin : begin + bc_part.size].reshape(bc_part.shape)
    return (
        output,
        input_grad,
        norm_gain_grad,
        z_share,
        x_share,
        bc_share,
        rest_share[:, 2 * STATE : 2 * STATE + heads],
        g_chan[:4],
        g_chan[4],
        g_bc[:4],
        g_bc[4],
        g_head[0],
        g_head[1],
        jnp.sum(g_chan[5].reshape(heads, HEAD), 1),
        g_chan[6],
        out_share,
    )


def solution(mesh):
    placed = (
        P("dp", None),
        P(),
        P(None, "tensor"),
        P(None, "tensor"),
        P(),
        P(None, "tensor"),
        P(None, "tensor"),
        P("tensor"),
        P(),
        P(),
        P("tensor"),
        P("tensor"),
        P("tensor"),
        P("tensor"),
        P("tensor", None),
        P("dp", None),
        P("dp"),
    )
    return jax.shard_map(
        partial(shards, mesh.shape["tensor"]),
        mesh=mesh,
        in_specs=placed,
        out_specs=(
            P("dp", None),
            P("dp", None),
            P(),
            P("dp", "tensor"),
            P("dp", "tensor"),
            P("dp", None),
            P("dp", "tensor"),
            P(None, "tensor"),
            P("tensor"),
            P(),
            P(),
            P("tensor"),
            P("tensor"),
            P("tensor"),
            P("tensor"),
            P("tensor", "dp"),
        ),
        check_vma=False,
    )
```
